768 devices in a mesh: row: 64 (over y, x, core), col: 12 (over z).
Axes of the slice: x: 4, y: 8, z: 12, core: 2. Of those that a mesh axis runs over, the one named last changes fastest.
Arguments:
- slab_amps: bfloat16 [64, 49152], P('row', 'col'), may hold values from -6 to 6
- lad_ints: bfloat16 [294912, 4096], P(('row', 'col')), may hold values from -0.0546875 to 0.0546875
- lad_pairs: int32 [294912], P(('row', 'col')), may hold values from 0 to 1535, as said below
- cycle_amps: bfloat16 [49152, 4096], P(('row', 'col')), may hold values from -6 to 6
- cycle_dest: int32 [49152, 1], P(('row', 'col')), may hold values from 0 to 63; in each aligned block of 64 rows (0 to 63, 64 to 127, ...) at most 2 rows name the same one
- cycle_block: int32 [49152], P(('row', 'col')), may hold values from 0 to 3
- cycle_kblk: int32 [49152], P(('row', 'col')), may hold values from 0 to 15
- cycle_ints: bfloat16 [12288, 1536], P('col'), may hold values from -0.0546875 to 0.0546875
Outputs:
- ladder_residual: float32 [64, 98304], P(None, ('row', 'col'))
- cycle_residual: float32 [16384, 1536], P('row', 'col')
The draws below stay inside these ranges and needn't reach their ends.
Inputs may be any that keep to these rules, and one draw needn't show every extreme that they name: `lad_pairs`: within each device's block of 384 entries the values are distinct; they encode p * 24 + q. `cycle_dest`: within the rows of one device (aligned blocks of 64) no owner is named by more than 2 rows.
All inputs are finite; a program needn't handle non-finite values.
Results may differ from the reference program's by a relative error of at most 0.0024.
Values may be sent and summed in bfloat16 or wider, within the bound.
A program may use at most 192 MiB of HBM per device.

```python
import math
import jax
import jax.numpy as jnp
import numpy as np
from jax import lax

TILE = 64
ROWS = 64
P_DEV = 64
Q_DEV = 24
W_DEV = 384
S_DEV = 64
M_DEV = 4
NK_DEV = 16
JB = 24
NP = 768
WSLOTS = 294912
TILES_ALL = 49152
CAP = 2
N_ROW = 64
N_COL = 12


def draw_lad_pairs(key, part):
    key = jax.random.fold_in(key, 11)
    pair_count = P_DEV * Q_DEV
    device_keys = jax.random.split(key, N_ROW * N_COL)

    def single(device_key):
        first_key, second_key = jax.random.split(device_key)
        middle = jax.random.permutation(first_key, pair_count - 2)[:W_DEV - 2] + 1
        chosen = jnp.concatenate([jnp.array([0, pair_count - 1], dtype=jnp.int32), middle.astype(jnp.int32)])
        return jax.random.permutation(second_key, chosen)
    return jax.vmap(single)(device_keys).reshape(-1).astype(jnp.int32)


def with_ends(entries, stream_key, least, top_value):
    index_at = [jax.random.randint(jax.random.fold_in(stream_key, axis), (), 0, length) for axis, length in enumerate(entries.shape)]
    widest = entries.shape.index(max(entries.shape))
    neighbour = index_at[:widest] + [(index_at[widest] + 1) % entries.shape[widest]] + index_at[widest + 1:]
    return entries.at[tuple(index_at)].set(least).at[tuple(neighbour)].set(top_value)


def block_levels(own_key, shape, cuts, low, largest):
    gain, own = 1.0, jax.random.fold_in(own_key, 6)
    for axis_at, blocks in cuts:
        draws = jnp.exp(jax.random.uniform(jax.random.fold_in(own, axis_at), (blocks,), jnp.float32, low / len(cuts), largest / len(cuts)))
        gain = gain * jnp.repeat(draws, shape[axis_at] // blocks).reshape([-1 if axis == axis_at else 1 for axis in range(len(shape))])
    return gain


def routed_block(own_key, own, number, rows, count, top, limit, slope):
    sequence = jax.random.permutation(own_key, count)
    crowded, common = shares(count, rows * top, limit, slope, True), shares(count, rows * top, limit, slope, False)
    places = jnp.arange(count)

    def named(sizes, offset_by):
        used = int((sizes > 0).sum())
        fixed = max(1, used // 4)
        shifted = fixed + (places - fixed + offset_by * (used - fixed)) % max(1, count - fixed)
        return jnp.zeros((count,), jnp.int32).at[sequence[jnp.where(places < fixed, places, shifted)]].set(jnp.asarray(sizes, jnp.int32))

    sizes = jnp.where(number % 4 == 0, named(crowded, number // 4), named(common, number - number // 4 - 1))
    mixed = jax.random.permutation(jax.random.fold_in(own, 3), count)
    donor, receiver = mixed[0:count // 2 * 2:2], mixed[1:count // 2 * 2:2]
    margin = jnp.minimum(sizes[donor] - 1, limit - sizes[receiver]) // 2
    margin = jnp.where((donor == sequence[0]) | (receiver == sequence[0]) | (sizes[receiver] == 0), 0, jnp.maximum(margin, 0))
    shifted = jax.random.randint(jax.random.fold_in(own, 4), (count // 2,), 0, 1 << 20) % (margin + 1)
    sizes = sizes.at[donor].add(-shifted).at[receiver].add(shifted)
    members = jnp.searchsorted(jnp.cumsum(sizes), jnp.arange(rows * top), side="right").astype(jnp.int32)
    grid = members.reshape(top, rows).T
    grid = grid[jax.random.permutation(jax.random.fold_in(own, 1), rows)]
    offset_by = jax.random.randint(jax.random.fold_in(own, 2), (rows, 1), 0, top)
    return jnp.take_along_axis(grid, (jnp.arange(top)[None, :] + offset_by) % top, axis=1)


def shares(number_of, total, most, lean, full):
    weights = [(1 << 20) // math.isqrt(grade ** lean) + 1 for grade in range(1, number_of + 1)]
    largest = most if full else min(most, max(-(-total // number_of), total * weights[0] // sum(weights)))
    least = 1 if total - largest >= number_of - 1 else 0
    given, surplus = [largest] + [least] * (number_of - 1), total - largest - least * (number_of - 1)
    while surplus > 0:
        movable = [i for i in range(1, number_of) if given[i] < largest] or [i for i in range(1, number_of) if given[i] < most]
        whole, budget = sum([weights[i] for i in movable]), surplus
        for i in movable:
            addition = min(most - given[i], max(1, budget * weights[i] // whole), surplus)
            given[i] = given[i] + addition
            surplus = surplus - addition
    return np.array(given)


def scatter_about(key, shape, deviation, bound, cuts=(), kind=jnp.bfloat16):
    loudness = block_levels(key, shape, cuts, -0.22, 0.18) if cuts else 1.0
    entries = jax.random.normal(key, shape, jnp.float32) * deviation * loudness
    return jnp.minimum(jnp.maximum(entries, -bound), bound).astype(kind)


def setup_inputs(seed: int = 0) -> dict:
    streams_of = jax.random.split(jax.random.key(seed), 9)
    slab_amps = scatter_about(streams_of[0], (ROWS, NP * TILE), 1.0, 6.0, ((0, 64), (1, 12)))
    lad_ints = scatter_about(streams_of[1], (WSLOTS, TILE * TILE), (N_COL * W_DEV * TILE // Q_DEV) ** -0.5, 0.0546875, ((0, 768),))
    lad_pairs = draw_lad_pairs(jax.random.fold_in(streams_of[8], 71), 0)
    cycle_amps = scatter_about(streams_of[3], (TILES_ALL, TILE * TILE), 1.0, 6.0, ((0, 768),))
    cycle_dest_keys = jax.random.split(jax.random.fold_in(streams_of[4], 1), TILES_ALL // S_DEV)
    cycle_dest_turns = jax.random.permutation(jax.random.fold_in(streams_of[4], 3), TILES_ALL // S_DEV)
    cycle_dest = jax.vmap(lambda own, number: routed_block(jax.random.fold_in(streams_of[4], 2), own, number, S_DEV, N_ROW, 1, CAP, 2))(cycle_dest_keys, cycle_dest_turns).reshape((TILES_ALL, 1))
    cycle_block = with_ends(jax.random.randint(streams_of[5], (TILES_ALL,), 0, M_DEV), jax.random.fold_in(streams_of[5], 1), 0, M_DEV - 1).astype(jnp.int32)
    cycle_kblk = with_ends(jax.random.randint(streams_of[6], (TILES_ALL,), 0, NK_DEV), jax.random.fold_in(streams_of[6], 1), 0, NK_DEV - 1).astype(jnp.int32)
    cycle_ints = scatter_about(streams_of[7], (N_COL * NK_DEV * TILE, JB * TILE), (N_COL * TILE * S_DEV // M_DEV) ** -0.5, 0.0546875, ((0, 12),))
    return {"slab_amps": slab_amps, "lad_ints": lad_ints, "lad_pairs": lad_pairs, "cycle_amps": cycle_amps, "cycle_dest": cycle_dest, "cycle_block": cycle_block, "cycle_kblk": cycle_kblk, "cycle_ints": cycle_ints}


def reference(slab_amps, lad_ints, lad_pairs, cycle_amps, cycle_dest, cycle_block, cycle_kblk, cycle_ints):
    amp_tiles = slab_amps.reshape(ROWS, N_COL, P_DEV, TILE).transpose(1, 2, 0, 3)
    weight_tiles = lad_ints.reshape(N_ROW, N_COL, W_DEV, TILE, TILE)
    pair_ids = lad_pairs.reshape(N_ROW, N_COL, W_DEV)

    def one_row(operands):
        weights, pair_row = operands
        p_block = pair_row // Q_DEV
        q_block = pair_row % Q_DEV
        chosen = jnp.take_along_axis(amp_tiles, p_block[:, :, None, None].astype(jnp.int32), axis=1)
        products = jnp.einsum('cskx,csxy->csky', chosen.astype(jnp.float32), weights.astype(jnp.float32),
                              precision=lax.Precision.HIGHEST)
        picker = (q_block[..., None] == jnp.arange(Q_DEV, dtype=jnp.int32)).astype(jnp.float32)
        return jnp.einsum('csq,csky->kqy', picker, products, precision=lax.Precision.HIGHEST)

    per_row = lax.map(one_row, (weight_tiles, pair_ids))
    ladder_residual = per_row.transpose(1, 0, 2, 3).reshape(ROWS, N_ROW * Q_DEV * TILE)

    owners = cycle_dest.reshape(N_ROW, N_COL, S_DEV)
    blocks = cycle_block.reshape(N_ROW, N_COL, S_DEV)
    columns = cycle_kblk.reshape(N_ROW, N_COL, S_DEV)
    col_ids = jnp.arange(N_COL, dtype=jnp.int32)[None, :, None]
    cell_index = ((owners * M_DEV + blocks) * N_COL + col_ids) * NK_DEV + columns
    cell_sums = jax.ops.segment_sum(cycle_amps.astype(jnp.float32), cell_index.reshape(-1).astype(jnp.int32),
                                    num_segments=N_ROW * M_DEV * N_COL * NK_DEV).astype(jnp.bfloat16)
    cycle_slab = cell_sums.reshape(N_ROW * M_DEV, N_COL * NK_DEV, TILE, TILE).transpose(0, 2, 1, 3)
    cycle_slab = cycle_slab.reshape(N_ROW * M_DEV * TILE, N_COL * NK_DEV * TILE)
    cycle_residual = jnp.dot(cycle_slab.astype(jnp.float32), cycle_ints.astype(jnp.float32),
                            precision=lax.Precision.HIGHEST)
    return ladder_residual, cycle_residual
```

```python
import jax
import jax.numpy as jnp
from jax import lax
from jax.experimental import pallas as pl
from jax.experimental.pallas import tpu as pltpu
from jax.sharding import PartitionSpec as P

MESH = pl.DeviceIdType.MESH
F32 = jnp.float32
BF16 = jnp.bfloat16
I32 = jnp.int32

NR = 64
NC = 12
NY, NX = 8, 4
TILES = 64
ENTRIES = 384
Q_DEV = 24
MSG = 48
SUB = 64
NSUB = 4
STEPS = 6


def dot(a, b):
    return jnp.dot(a, b, preferred_element_type=F32)


def iota(shape, dim):
    return lax.broadcasted_iota(I32, shape, dim)


def kernel(
    amps_ref, pairs_ref, dest_ref, block_ref, kblk_ref, w_hbm, cyc_hbm, b_hbm,
    lad_out, cyc_out,
    w_ref, cyc_ref, b_ref, stage, outgoing, arrived, gather, gstage, lad_lhs, placer, dense,
    lad_part, lad_slots, cells, cyc_lhs, part, slot_up, slot_dn, turn,
    local_sem, g1_send, g1_recv, g2_send, g2_recv, a_send, a_recv, l_send, l_recv,
    r_send, r_recv_up, r_recv_dn,
):
    me = lax.axis_index("row")
    col = lax.axis_index("col")
    my_y = me // 8
    my_x = lax.rem(me // 2, 4)
    my_core = lax.rem(me, 2)
    my_slot = my_y * 2 + my_core

    local = [
        pltpu.make_async_copy(cyc_hbm, cyc_ref, local_sem.at[0]),
        pltpu.make_async_copy(w_hbm, w_ref, local_sem.at[1]),
        pltpu.make_async_copy(b_hbm, b_ref, local_sem.at[2]),
    ]
    for copy in local:
        copy.start()

    barrier = pltpu.get_barrier_semaphore()

    def greet_row(k, carry):
        pl.semaphore_signal(
            barrier, inc=1, device_id={"row": lax.rem(me + k, NR)}, device_id_type=MESH
        )
        return carry

    def greet_col(k, carry):
        pl.semaphore_signal(
            barrier, inc=1, device_id={"col": lax.rem(col + k, NC)}, device_id_type=MESH
        )
        return carry

    lax.fori_loop(1, NR, greet_row, 0)
    lax.fori_loop(1, NC, greet_col, 0)

    flipped = amps_ref[...].astype(F32).T
    turn[:, 0:32] = flipped[0:64, :]
    turn[:, 32:64] = flipped[64:128, :]
    quarter = [[turn[pl.ds(2 * a1 + par, 16, stride=4), :] for a1 in (0, 1)] for par in (0, 1)]
    message = jnp.concatenate([jnp.concatenate(quarter[par], axis=1) for par in (0, 1)], axis=0)

    dest_col = dest_ref[...]
    eye = iota((TILES, TILES), 0) == iota((TILES, TILES), 1)
    dest_row = jnp.sum(jnp.where(eye, dest_col, 0), axis=0, keepdims=True)
    same = dest_col == dest_row
    earlier_col = iota((TILES, TILES), 0) < iota((TILES, TILES), 1)
    earlier_row = iota((TILES, TILES), 1) < iota((TILES, TILES), 0)
    pos_row = jnp.sum(jnp.where(same & earlier_col, 1, 0), axis=0, keepdims=True)
    pos_col = jnp.sum(jnp.where(same & earlier_row, 1, 0), axis=1, keepdims=True)
    code_row = block_ref[...] * 16 + kblk_ref[...]
    code_col = jnp.sum(jnp.where(eye, code_row, 0), axis=1, keepdims=True)
    slot_row = dest_row * 2 + pos_row
    slot_col = dest_col * 2 + pos_col
    chosen = (iota((2 * NR, TILES), 0) == slot_row).astype(F32).astype(BF16)
    codes = jnp.sum(
        jnp.where(iota((TILES, 2 * NR), 1) == slot_col, code_col + 1, 0), axis=0, keepdims=True
    ) - 1
    gather[my_x, my_slot, 0:32, :] = message.astype(BF16)
    gather[my_x, my_slot, 32:48, :] = jnp.where(
        iota((16, 128), 0) == 0, codes, 0
    ).astype(F32).astype(BF16)

    pl.semaphore_wait(barrier, NR - 1 + NC - 1)

    def first_stage(k):
        there = lax.rem(my_slot + k, 16)
        row = (there // 2) * 8 + my_x * 2 + lax.rem(there, 2)
        return there, pltpu.make_async_remote_copy(
            gather.at[my_x, my_slot], gather.at[my_x, my_slot], g1_send.at[k], g1_recv.at[my_slot],
            device_id={"row": row}, device_id_type=MESH,
        )

    def first_send(k, carry):
        first_stage(k)[1].start()
        return carry

    lax.fori_loop(1, 16, first_send, 0)

    local[0].wait()

    def stage_tiles(g, carry):
        picked = dot(chosen, cyc_ref[:, pl.ds(pl.multiple_of(g * 256, 256), 256)])
        stage[pl.ds(2 * g, 128, stride=32), :] = picked[:, 0:128]
        stage[pl.ds(2 * g + 1, 128, stride=32), :] = picked[:, 128:256]
        return carry

    lax.fori_loop(0, 16, stage_tiles, 0)

    def tile_copy(d):
        return pltpu.make_async_remote_copy(
            outgoing.at[d], arrived.at[me], a_send.at[d], a_recv.at[me],
            device_id={"row": d}, device_id_type=MESH,
        )

    def tile_send(k, carry):
        d = lax.rem(me + k, NR)
        outgoing[d] = stage[pl.ds(pl.multiple_of(d * 64, 64), 64), :].astype(BF16)
        tile_copy(d).start()
        return carry

    lax.fori_loop(1, NR, tile_send, 0)
    arrived[me] = stage[pl.ds(pl.multiple_of(me * 64, 64), 64), :].astype(BF16)

    def first_wait(k, carry):
        there = lax.rem(my_slot + k, 16)
        pltpu.make_async_remote_copy(
            gather.at[my_x, there], gather.at[my_x, there], g1_send.at[0], g1_recv.at[there],
            device_id={"row": lax.rem(me + 1, NR)}, device_id_type=MESH,
        ).wait_recv()
        return carry

    lax.fori_loop(1, 16, first_wait, 0)

    def second_copy(k, x):
        there = lax.rem(my_x + k, NX)
        return pltpu.make_async_remote_copy(
            gather.at[x], gather.at[x], g2_send.at[k], g2_recv.at[x],
            device_id={"row": my_y * 8 + there * 2 + my_core}, device_id_type=MESH,
        )

    for k in range(1, NX):
        second_copy(k, my_x).start()

    pairs = pairs_ref[...]
    p_at = iota((64, ENTRIES), 0)
    p_code = (2 * lax.rem(p_at, 32) + p_at // 32) * Q_DEV

    def build(q, carry):
        placer[pl.ds(pl.multiple_of(q * 64, 64), 64), :] = (
            (p_code + q == pairs).astype(F32).astype(BF16)
        )
        return carry

    lax.fori_loop(0, Q_DEV, build, 0)
    local[1].wait()

    def place(g, carry):
        w_part = w_ref[:, pl.ds(pl.multiple_of(g * 256, 256), 256)]
        for quarter_at in range(4):
            placed = dot(placer[quarter_at * 384:(quarter_at + 1) * 384, :], w_part).astype(BF16)
            for j in range(6):
                q = quarter_at * 6 + j
                for i in (0, 1):
                    dense[
                        q // 2, pl.ds(pl.multiple_of((2 * g + i) * 64, 64), 64),
                        (q % 2) * 128:(q % 2 + 1) * 128,
                    ] = placed[j * 64:(j + 1) * 64, i * 128:(i + 1) * 128]
        return carry

    lax.fori_loop(0, 16, place, 0)

    for k in range(1, NX):
        x = lax.rem(my_x + k, NX)
        second_copy(k, x).wait_recv()

    def widen(i, carry):
        x, rest = i // 16, lax.rem(i, 16)
        row = (rest // 2) * 8 + x * 2 + lax.rem(rest, 2)
        gstage[pl.ds(pl.multiple_of(row * MSG, MSG), MSG), :] = gather[x, rest].astype(F32)
        return carry

    lax.fori_loop(0, NR, widen, 0)
    for par in (0, 1):
        for b in range(16):
            lad_lhs[par * 64:(par + 1) * 64, b * 128:(b + 1) * 128] = (
                gstage[pl.ds(par * 16 + b, NR, stride=MSG), :].astype(BF16)
            )

    low = iota((64, 128), 1) < 64

    def lad_copy(k):
        c = lax.rem(col + k, NC)
        return pltpu.make_async_remote_copy(
            lad_part.at[c], lad_slots.at[k], l_send.at[k], l_recv.at[k],
            device_id={"col": c}, device_id_type=MESH,
        )

    def ladder(k):
        c = lax.rem(col + k, NC)
        acc = dot(lad_lhs[...], dense[c])
        first = acc[0:64, 0:128] + pltpu.roll(acc[64:128, 0:128], 64, 1)
        second = pltpu.roll(acc[0:64, 128:256], 64, 1) + acc[64:128, 128:256]
        lad_part[c] = jnp.where(low, first, second)

    def ladder_send(k, carry):
        ladder(k)
        lad_copy(k).start()
        return carry

    lax.fori_loop(1, NC, ladder_send, 0)
    ladder(0)

    all_codes = gstage[pl.ds(32, NR, stride=MSG), :]
    mine = []
    for j in (0, 1):
        here = jnp.where(iota((NR, 128), 1) == 2 * me + j, all_codes, 0.0)
        mine.append(jnp.sum(here, axis=1, keepdims=True))
    slot_codes = jnp.concatenate(mine, axis=0)
    put = (slot_codes == iota((2 * NR, 128), 1).astype(F32)).astype(F32).T[0:64, :].astype(BF16)

    def tile_wait(k, carry):
        s = lax.rem(me + NR - k, NR)
        pltpu.make_async_remote_copy(
            outgoing.at[s], arrived.at[s], a_send.at[s], a_recv.at[s],
            device_id={"row": lax.rem(me + k, NR)}, device_id_type=MESH,
        ).wait_recv()
        stage[pl.ds(pl.multiple_of(s * 64, 64), 64), :] = arrived[s].astype(F32)
        return carry

    stage[pl.ds(pl.multiple_of(me * 64, 64), 64), :] = arrived[me].astype(F32)
    lax.fori_loop(1, NR, tile_wait, 0)

    def cell(g, carry):
        wide = []
        for i in (0, 1):
            a = 2 * g + i
            wide.append(jnp.concatenate(
                [stage[pl.ds(a + 32 * j, NR, stride=64), :] for j in (0, 1)], axis=0
            ).astype(BF16))
        summed = dot(put, jnp.concatenate(wide, axis=1))
        cells[pl.ds(2 * g, 64, stride=32), :] = summed[:, 0:128]
        cells[pl.ds(2 * g + 1, 64, stride=32), :] = summed[:, 128:256]
        return carry

    lax.fori_loop(0, 16, cell, 0)

    low32 = iota((32, 128), 1) < 64

    def pair(i, carry):
        m, nn = i // 8, lax.rem(i, 8)
        at = pl.multiple_of((m * 16 + 2 * nn) * 32, 32)
        even = cells[pl.ds(at, 32), :]
        odd = cells[pl.ds(pl.multiple_of(at + 32, 32), 32), :]
        lanes = pl.ds(pl.multiple_of(nn * 128, 128), 128)
        cyc_lhs[pl.ds(pl.multiple_of(m * 32, 32), 32), lanes] = jnp.where(
            low32, even, pltpu.roll(odd, 64, 1)
        ).astype(BF16)
        cyc_lhs[pl.ds(pl.multiple_of(128 + m * 32, 32), 32), lanes] = jnp.where(
            low32, pltpu.roll(even, 64, 1), odd
        ).astype(BF16)
        return carry

    lax.fori_loop(0, 32, pair, 0)
    local[2].wait()

    def product(c):
        lanes = pl.ds(pl.multiple_of(c * 128, 128), 128)
        made = dot(cyc_lhs[...], b_ref[:, lanes])
        for u in range(NSUB):
            part[c, u] = made[u * SUB:(u + 1) * SUB, :]

    up, dn = lax.rem(col + 1, NC), lax.rem(col + NC - 1, NC)
    arms = ((up, slot_up, r_recv_up), (dn, slot_dn, r_recv_dn))

    def target(t, arm):
        return lax.rem(col + (STEPS - t if arm == 0 else NC - STEPS + t), NC)

    def pieces(t, arm):
        if t:
            return range(NSUB)
        return (0, 1) if arm == 0 else (2, 3)

    def ring_copy(t, arm, u):
        device, slots, recv = arms[arm]
        return pltpu.make_async_remote_copy(
            part.at[target(t, arm), u], slots.at[t, u], r_send.at[t, arm, u], recv.at[t, u],
            device_id={"col": device}, device_id_type=MESH,
        )

    product(target(0, 0))
    for arm in (0, 1):
        for u in pieces(0, arm):
            ring_copy(0, arm, u).start()
    for t in range(1, STEPS):
        for arm in (0, 1):
            product(target(t, arm))
        for i in range(NSUB):
            for arm in (0, 1):
                u = i if arm == 0 else (i + 2) % 4
                if u in pieces(t - 1, arm):
                    ring_copy(t - 1, arm, u).wait_recv()
                    c = target(t, arm)
                    part[c, u] = part[c, u] + arms[arm][1][t - 1, u]
                ring_copy(t, arm, u).start()
    product(col)

    def lad_wait(k, carry):
        lad_copy(k).wait_recv()
        return carry

    lax.fori_loop(1, NC, lad_wait, 0)
    total = lad_part[col]
    for k in range(1, NC):
        total = total + lad_slots[k]
    lad_out[...] = total

    for u in range(NSUB):
        for arm in (0, 1):
            ring_copy(STEPS - 1, arm, u).wait_recv()
        par, half = u // 2, u % 2
        cyc_out[pl.ds(par + half * 128, SUB, stride=2), :] = (
            part[col, u] + slot_up[STEPS - 1, u] + slot_dn[STEPS - 1, u]
        )

    def first_sent(k, carry):
        first_stage(k)[1].wait_send()
        return carry

    def tile_sent(k, carry):
        tile_copy(lax.rem(me + k, NR)).wait_send()
        return carry

    def lad_sent(k, carry):
        lad_copy(k).wait_send()
        return carry

    lax.fori_loop(1, 16, first_sent, 0)
    for k in range(1, NX):
        second_copy(k, my_x).wait_send()
    lax.fori_loop(1, NR, tile_sent, 0)
    lax.fori_loop(1, NC, lad_sent, 0)
    for t in range(STEPS):
        for arm in (0, 1):
            for u in pieces(t, arm):
                ring_copy(t, arm, u).wait_send()


def local(
    slab_amps, lad_ints, lad_pairs, cycle_amps, cycle_dest, cycle_block, cycle_kblk, cycle_ints
):
    vmem = pl.BlockSpec(memory_space=pltpu.VMEM)
    hbm = pl.BlockSpec(memory_space=pl.ANY)
    dma = pltpu.SemaphoreType.DMA
    return pl.pallas_call(
        kernel,
        out_shape=(
            jax.ShapeDtypeStruct((64, 128), F32),
            jax.ShapeDtypeStruct((256, 128), F32),
        ),
        in_specs=[vmem] * 5 + [hbm] * 3,
        out_specs=(vmem, vmem),
        scratch_shapes=[
            pltpu.VMEM((ENTRIES, 4096), BF16),
            pltpu.VMEM((TILES, 4096), BF16),
            pltpu.VMEM((1024, 1536), BF16),
            pltpu.VMEM((4096, 128), F32),
            pltpu.VMEM((NR, 64, 128), BF16),
            pltpu.VMEM((NR, 64, 128), BF16),
            pltpu.VMEM((NX, 16, MSG, 128), BF16),
            pltpu.VMEM((NR * MSG, 128), F32),
            pltpu.VMEM((128, 2048), BF16),
            pltpu.VMEM((Q_DEV * 64, ENTRIES), BF16),
            pltpu.VMEM((NC, 2048, 256), BF16),
            pltpu.VMEM((NC, 64, 128), F32),
            pltpu.VMEM((NC, 64, 128), F32),
            pltpu.VMEM((2048, 128), F32),
            pltpu.VMEM((256, 1024), BF16),
            pltpu.VMEM((NC, NSUB, SUB, 128), F32),
            pltpu.VMEM((STEPS, NSUB, SUB, 128), F32),
            pltpu.VMEM((STEPS, NSUB, SUB, 128), F32),
            pltpu.VMEM((64, 64), F32),
            dma((3,)),
            dma((16,)), dma((16,)),
            dma((NX,)), dma((NX,)),
            dma((NR,)), dma((NR,)),
            dma((NC,)), dma((NC,)),
            dma((STEPS, 2, NSUB)), dma((STEPS, NSUB)), dma((STEPS, NSUB)),
        ],
        name="ladder_and_cycle",
        compiler_params=pltpu.CompilerParams(
            collective_id=0, has_side_effects=True, vmem_limit_bytes=52 << 20
        ),
    )(
        slab_amps.reshape(32, 128), lad_pairs.reshape(1, ENTRIES), cycle_dest,
        cycle_block.reshape(1, TILES), cycle_kblk.reshape(1, TILES),
        lad_ints, cycle_amps, cycle_ints,
    )


def solution(mesh):
    in_specs = (
        P("row", "col"),
        P(("row", "col"), None),
        P(("row", "col")),
        P(("row", "col"), None),
        P(("row", "col"), None),
        P(("row", "col")),
        P(("row", "col")),
        P("col", None),
    )
    out_specs = (P(None, ("row", "col")), P("row", "col"))
    return jax.shard_map(local, mesh=mesh, in_specs=in_specs, out_specs=out_specs, check_vma=False)
```

```python
import jax
import jax.numpy as jnp
from jax import lax
from jax.experimental import pallas as pl
from jax.experimental.pallas import tpu as pltpu
from jax.sharding import PartitionSpec as P

MESH = pl.DeviceIdType.MESH
F32 = jnp.float32
BF16 = jnp.bfloat16
I32 = jnp.int32

NR = 64
NC = 12
NY, NX = 8, 4
TILES = 64
ENTRIES = 384
Q_DEV = 24
MSG = 48
SUB = 64
NSUB = 4
STEPS = 6
LADDER_ORDER = (6, 5, 7, 4, 8, 3, 9, 2, 10, 1, 11)
LOW = 3
FIRST = 33
PLACED = 8


def dot(a, b):
    return jnp.dot(a, b, preferred_element_type=F32)


def iota(shape, dim):
    return lax.broadcasted_iota(I32, shape, dim)


def kernel(
    amps_hbm, pairs_hbm, dest_hbm, block_hbm, kblk_hbm, w_hbm, cyc_hbm, b_hbm,
    lad_out, cyc_out,
    amps_ref, pairs_ref, dest_ref, block_ref, kblk_ref,
    w_ref, cyc_ref, b_ref, stage, outgoing, arrived, gather, gstage, lad_lhs, placer, dense,
    lad_part, lad_low, lad_slots, cells, cyc_lhs, part, slot_up, slot_dn, low_out, low_in, turn, lines,
    local_sem, g1_send, g1_recv, g2_send, g2_recv, g3_send, g3_recv, a_send, a_recv, l_send, l_recv,
    r_send, r_recv_up, r_recv_dn,
):
    me = lax.axis_index("row")
    col = lax.axis_index("col")
    my_y = me // 8
    my_x = lax.rem(me // 2, 4)
    my_core = lax.rem(me, 2)

    barrier = pltpu.get_barrier_semaphore()

    def away(i):
        half = i // 2
        return 32 + half - 2 * half * lax.rem(i, 2)

    def greet_row(i, carry):
        pl.semaphore_signal(
            barrier, inc=1, device_id={"row": lax.rem(me + away(i), NR)}, device_id_type=MESH
        )
        return carry

    def greet_col(k, carry):
        pl.semaphore_signal(
            barrier, inc=1, device_id={"col": lax.rem(col + k, NC)}, device_id_type=MESH
        )
        return carry

    lax.fori_loop(1, NR, greet_row, 0)
    lax.fori_loop(1, NC, greet_col, 0)

    local = [
        pltpu.make_async_copy(cyc_hbm, cyc_ref, local_sem.at[0]),
        pltpu.make_async_copy(w_hbm, w_ref, local_sem.at[1]),
        pltpu.make_async_copy(b_hbm, b_ref, local_sem.at[2]),
        pltpu.make_async_copy(dest_hbm, dest_ref, local_sem.at[3]),
        pltpu.make_async_copy(block_hbm, block_ref, local_sem.at[4]),
        pltpu.make_async_copy(kblk_hbm, kblk_ref, local_sem.at[5]),
        pltpu.make_async_copy(amps_hbm, amps_ref, local_sem.at[6]),
        pltpu.make_async_copy(pairs_hbm, pairs_ref, local_sem.at[7]),
    ]
    for i in (3, 4, 5, 6, 0, 7, 1, 2):
        local[i].start()

    local[6].wait()
    for i in range(32):
        lines[i:i + 1, :] = amps_ref[:, i * 128:(i + 1) * 128].astype(F32)
    flipped = lines[...].T
    turn[:, 0:32] = flipped[0:64, :]
    turn[:, 32:64] = flipped[64:128, :]
    quarter = [[turn[pl.ds(2 * a1 + par, 16, stride=4), :] for a1 in (0, 1)] for par in (0, 1)]
    message = jnp.concatenate([jnp.concatenate(quarter[par], axis=1) for par in (0, 1)], axis=0)

    for i in (3, 4, 5):
        local[i].wait()
    dest_row = dest_ref[...]
    eye = iota((TILES, TILES), 0) == iota((TILES, TILES), 1)
    dest_col = jnp.sum(jnp.where(eye, dest_row, 0), axis=1, keepdims=True)
    same = dest_col == dest_row
    earlier_col = iota((TILES, TILES), 0) < iota((TILES, TILES), 1)
    earlier_row = iota((TILES, TILES), 1) < iota((TILES, TILES), 0)
    pos_row = jnp.sum(jnp.where(same & earlier_col, 1, 0), axis=0, keepdims=True)
    pos_col = jnp.sum(jnp.where(same & earlier_row, 1, 0), axis=1, keepdims=True)
    code_row = (block_ref[...] * 16 + kblk_ref[...]).reshape(1, TILES)
    code_col = jnp.sum(jnp.where(eye, code_row, 0), axis=1, keepdims=True)
    slot_row = dest_row * 2 + pos_row
    slot_col = dest_col * 2 + pos_col
    chosen = (iota((2 * NR, TILES), 0) == slot_row).astype(F32).astype(BF16)
    codes = jnp.sum(
        jnp.where(iota((TILES, 2 * NR), 1) == slot_col, code_col + 1, 0), axis=0, keepdims=True
    ) - 1
    gather[my_core, my_x, my_y, 0:32, :] = message.astype(BF16)
    gather[my_core, my_x, my_y, 32:48, :] = jnp.where(
        iota((16, 128), 0) == 0, codes, 0
    ).astype(F32).astype(BF16)

    local[0].wait()

    def stage_tiles(g, carry):
        picked = dot(chosen, cyc_ref[:, pl.ds(pl.multiple_of(g * 256, 256), 256)])
        stage[pl.ds(2 * g, 128, stride=32), :] = picked[:, 0:128]
        stage[pl.ds(2 * g + 1, 128, stride=32), :] = picked[:, 128:256]
        return carry

    lax.fori_loop(0, 16, stage_tiles, 0, unroll=4)

    def tile_fill(d, carry):
        outgoing[d] = stage[pl.ds(pl.multiple_of(d * 64, 64), 64), :].astype(BF16)
        return carry

    lax.fori_loop(0, NR, tile_fill, 0, unroll=4)
    arrived[me] = stage[pl.ds(pl.multiple_of(me * 64, 64), 64), :].astype(BF16)

    def tile_copy(d):
        return pltpu.make_async_remote_copy(
            outgoing.at[d], arrived.at[me], a_send.at[d], a_recv.at[me],
            device_id={"row": d}, device_id_type=MESH,
        )

    def tile_send(i, carry):
        tile_copy(lax.rem(me + away(i), NR)).start()
        return carry

    def first_copy(k, y):
        there = lax.rem(my_y + k, NY)
        ref = gather.at[my_core, my_x, y]
        return pltpu.make_async_remote_copy(
            ref, ref, g1_send.at[k], g1_recv.at[y],
            device_id={"row": there * 8 + my_x * 2 + my_core}, device_id_type=MESH,
        )

    def second_copy(k, x):
        there = lax.rem(my_x + k, NX)
        ref = gather.at[my_core, x]
        return pltpu.make_async_remote_copy(
            ref, ref, g2_send.at[k], g2_recv.at[x],
            device_id={"row": my_y * 8 + there * 2 + my_core}, device_id_type=MESH,
        )

    def third_copy(core):
        ref = gather.at[core]
        return pltpu.make_async_remote_copy(
            ref, ref, g3_send.at[0], g3_recv.at[0],
            device_id={"row": me + 1 - 2 * my_core}, device_id_type=MESH,
        )

    pl.semaphore_wait(barrier, NR - 1 + NC - 1)
    for k in (4, 3, 5, 2, 6, 1, 7):
        first_copy(k, my_y).start()
    lax.fori_loop(1, FIRST, tile_send, 0)

    local[7].wait()
    pairs = pairs_ref[...].reshape(1, ENTRIES)
    p_at = iota((64, ENTRIES), 0)
    p_code = (2 * lax.rem(p_at, 32) + p_at // 32) * Q_DEV

    def build(q, carry):
        placer[pl.ds(pl.multiple_of(q * 64, 64), 64), :] = (
            (p_code + q == pairs).astype(F32).astype(BF16)
        )
        return carry

    lax.fori_loop(0, Q_DEV, build, 0)
    local[1].wait()

    def place(g, carry):
        w_part = w_ref[:, pl.ds(pl.multiple_of(g * 256, 256), 256)]
        for quarter_at in range(4):
            placed = dot(placer[quarter_at * 384:(quarter_at + 1) * 384, :], w_part).astype(BF16)
            for j in range(6):
                q = quarter_at * 6 + j
                for i in (0, 1):
                    dense[
                        q // 2, pl.ds(pl.multiple_of((2 * g + i) * 64, 64), 64),
                        (q % 2) * 128:(q % 2 + 1) * 128,
                    ] = placed[j * 64:(j + 1) * 64, i * 128:(i + 1) * 128]
        return carry

    lax.fori_loop(0, PLACED, place, 0, unroll=2)

    for k in range(1, NY):
        first_copy(k, lax.rem(my_y + k, NY)).wait_recv()
    for k in (2, 1, 3):
        second_copy(k, my_x).start()
    lax.fori_loop(FIRST, NR, tile_send, 0)
    lax.fori_loop(PLACED, 16, place, 0, unroll=2)
    for k in range(1, NX):
        second_copy(k, lax.rem(my_x + k, NX)).wait_recv()
    third_copy(my_core).start()
    third_copy(1 - my_core).wait_recv()

    def widen(i, carry):
        core, x, y = i // 32, lax.rem(i // 8, NX), lax.rem(i, NY)
        row = y * 8 + x * 2 + core
        gstage[pl.ds(pl.multiple_of(row * MSG, MSG), MSG), :] = gather[core, x, y].astype(F32)
        return carry

    lax.fori_loop(0, NR, widen, 0, unroll=4)
    for par in (0, 1):
        for b in range(16):
            lad_lhs[par * 64:(par + 1) * 64, b * 128:(b + 1) * 128] = (
                gstage[pl.ds(par * 16 + b, NR, stride=MSG), :].astype(BF16)
            )

    low = iota((64, 128), 1) < 64

    def lad_copy(k):
        c = lax.rem(col + k, NC)
        return pltpu.make_async_remote_copy(
            lad_low.at[c], lad_slots.at[k], l_send.at[k], l_recv.at[k],
            device_id={"col": c}, device_id_type=MESH,
        )

    def ladder(k):
        c = lax.rem(col + k, NC)
        acc = dot(lad_lhs[...], dense[c])
        first = acc[0:64, 0:128] + pltpu.roll(acc[64:128, 0:128], 64, 1)
        second = pltpu.roll(acc[0:64, 128:256], 64, 1) + acc[64:128, 128:256]
        total = jnp.where(low, first, second)
        if k == 0:
            lad_part[...] = total
        else:
            lad_low[c] = total.astype(BF16)

    def ladder_send(k):
        ladder(k)
        lad_copy(k).start()

    for k in LADDER_ORDER:
        ladder_send(k)
    ladder(0)

    all_codes = gstage[pl.ds(32, NR, stride=MSG), :]
    mine = []
    for j in (0, 1):
        here = jnp.where(iota((NR, 128), 1) == 2 * me + j, all_codes, 0.0)
        mine.append(jnp.sum(here, axis=1, keepdims=True))
    slot_codes = jnp.concatenate(mine, axis=0)
    put = (slot_codes == iota((2 * NR, 128), 1).astype(F32)).astype(F32).T[0:64, :].astype(BF16)

    def tile_wait(i, carry):
        k = away(i)
        s = lax.rem(me + NR - k, NR)
        pltpu.make_async_remote_copy(
            outgoing.at[s], arrived.at[s], a_send.at[s], a_recv.at[s],
            device_id={"row": lax.rem(me + k, NR)}, device_id_type=MESH,
        ).wait_recv()
        stage[pl.ds(pl.multiple_of(s * 64, 64), 64), :] = arrived[s].astype(F32)
        return carry

    stage[pl.ds(pl.multiple_of(me * 64, 64), 64), :] = arrived[me].astype(F32)
    lax.fori_loop(1, NR, tile_wait, 0)

    def cell(g, carry):
        wide = []
        for i in (0, 1):
            a = 2 * g + i
            wide.append(jnp.concatenate(
                [stage[pl.ds(a + 32 * j, NR, stride=64), :] for j in (0, 1)], axis=0
            ).astype(BF16))
        summed = dot(put, jnp.concatenate(wide, axis=1))
        cells[pl.ds(2 * g, 64, stride=32), :] = summed[:, 0:128]
        cells[pl.ds(2 * g + 1, 64, stride=32), :] = summed[:, 128:256]
        return carry

    lax.fori_loop(0, 16, cell, 0, unroll=8)

    low32 = iota((32, 128), 1) < 64

    def pair(i, carry):
        m, nn = i // 8, lax.rem(i, 8)
        at = pl.multiple_of((m * 16 + 2 * nn) * 32, 32)
        even = cells[pl.ds(at, 32), :]
        odd = cells[pl.ds(pl.multiple_of(at + 32, 32), 32), :]
        lanes = pl.ds(pl.multiple_of(nn * 128, 128), 128)
        cyc_lhs[pl.ds(pl.multiple_of(m * 32, 32), 32), lanes] = jnp.where(
            low32, even, pltpu.roll(odd, 64, 1)
        ).astype(BF16)
        cyc_lhs[pl.ds(pl.multiple_of(128 + m * 32, 32), 32), lanes] = jnp.where(
            low32, pltpu.roll(even, 64, 1), odd
        ).astype(BF16)
        return carry

    lax.fori_loop(0, 32, pair, 0, unroll=8)
    local[2].wait()

    def product(c):
        lanes = pl.ds(pl.multiple_of(c * 128, 128), 128)
        made = dot(cyc_lhs[...], b_ref[:, lanes])
        for u in range(NSUB):
            part[c, u] = made[u * SUB:(u + 1) * SUB, :]

    up, dn = lax.rem(col + 1, NC), lax.rem(col + NC - 1, NC)
    arms = ((up, slot_up, r_recv_up), (dn, slot_dn, r_recv_dn))

    def target(t, arm):
        return lax.rem(col + (STEPS - t if arm == 0 else NC - STEPS + t), NC)

    def pieces(t, arm):
        if t:
            return range(NSUB)
        return (0, 1) if arm == 0 else (2, 3)

    def ring_copy(t, arm, u):
        device, slots, recv = arms[arm]
        if t < LOW:
            source, landing = low_out.at[t, arm, u], low_in.at[t, arm, u]
        else:
            source, landing = part.at[target(t, arm), u], slots.at[t - LOW, u]
        return pltpu.make_async_remote_copy(
            source, landing, r_send.at[t, arm, u], recv.at[t, u],
            device_id={"col": device}, device_id_type=MESH,
        )

    def ring_send(t, arm, u):
        if t < LOW:
            low_out[t, arm, u] = part[target(t, arm), u].astype(BF16)
        ring_copy(t, arm, u).start()

    def landed(t, arm, u):
        ring_copy(t, arm, u).wait_recv()
        return low_in[t, arm, u].astype(F32) if t < LOW else arms[arm][1][t - LOW, u]

    product(target(0, 0))
    for arm in (0, 1):
        for u in pieces(0, arm):
            ring_send(0, arm, u)
    for t in range(1, STEPS):
        for arm in (0, 1):
            product(target(t, arm))
        for i in range(NSUB):
            for arm in (0, 1):
                u = i if arm == 0 else (i + 2) % 4
                if u in pieces(t - 1, arm):
                    c = target(t, arm)
                    part[c, u] = part[c, u] + landed(t - 1, arm, u)
                ring_send(t, arm, u)
    product(col)

    def lad_wait(k, carry):
        lad_copy(k).wait_recv()
        return carry

    lax.fori_loop(1, NC, lad_wait, 0)
    total = lad_part[...]
    for k in range(1, NC):
        total = total + lad_slots[k].astype(F32)
    lad_out[...] = total

    for u in range(NSUB):
        par, half = u // 2, u % 2
        cyc_out[pl.ds(par + half * 128, SUB, stride=2), :] = (
            part[col, u] + landed(STEPS - 1, 0, u) + landed(STEPS - 1, 1, u)
        )

    def tile_sent(k, carry):
        tile_copy(lax.rem(me + k, NR)).wait_send()
        return carry

    def lad_sent(k, carry):
        lad_copy(k).wait_send()
        return carry

    for k in range(1, NY):
        first_copy(k, my_y).wait_send()
    for k in range(1, NX):
        second_copy(k, my_x).wait_send()
    third_copy(my_core).wait_send()
    lax.fori_loop(1, NR, tile_sent, 0)
    lax.fori_loop(1, NC, lad_sent, 0)
    for t in range(STEPS):
        for arm in (0, 1):
            for u in pieces(t, arm):
                ring_copy(t, arm, u).wait_send()


def local(
    slab_amps, lad_ints, lad_pairs, cycle_amps, cycle_dest, cycle_block, cycle_kblk, cycle_ints
):
    vmem = pl.BlockSpec(memory_space=pltpu.VMEM)
    hbm = pl.BlockSpec(memory_space=pl.ANY)
    dma = pltpu.SemaphoreType.DMA
    return pl.pallas_call(
        kernel,
        out_shape=(
            jax.ShapeDtypeStruct((64, 128), F32),
            jax.ShapeDtypeStruct((256, 128), F32),
        ),
        in_specs=[hbm] * 8,
        out_specs=(vmem, vmem),
        scratch_shapes=[
            pltpu.VMEM((1, 4096), BF16),
            pltpu.VMEM((ENTRIES,), I32),
            pltpu.VMEM((1, TILES), I32),
            pltpu.VMEM((TILES,), I32),
            pltpu.VMEM((TILES,), I32),
            pltpu.VMEM((ENTRIES, 4096), BF16),
            pltpu.VMEM((TILES, 4096), BF16),
            pltpu.VMEM((1024, 1536), BF16),
            pltpu.VMEM((4096, 128), F32),
            pltpu.VMEM((NR, 64, 128), BF16),
            pltpu.VMEM((NR, 64, 128), BF16),
            pltpu.VMEM((2, NX, NY, MSG, 128), BF16),
            pltpu.VMEM((NR * MSG, 128), F32),
            pltpu.VMEM((128, 2048), BF16),
            pltpu.VMEM((Q_DEV * 64, ENTRIES), BF16),
            pltpu.VMEM((NC, 2048, 256), BF16),
            pltpu.VMEM((64, 128), F32),
            pltpu.VMEM((NC, 64, 128), BF16),
            pltpu.VMEM((NC, 64, 128), BF16),
            pltpu.VMEM((2048, 128), F32),
            pltpu.VMEM((256, 1024), BF16),
            pltpu.VMEM((NC, NSUB, SUB, 128), F32),
            pltpu.VMEM((STEPS - LOW, NSUB, SUB, 128), F32),
            pltpu.VMEM((STEPS - LOW, NSUB, SUB, 128), F32),
            pltpu.VMEM((max(LOW, 1), 2, NSUB, SUB, 128), BF16),
            pltpu.VMEM((max(LOW, 1), 2, NSUB, SUB, 128), BF16),
            pltpu.VMEM((64, 64), F32),
            pltpu.VMEM((32, 128), F32),
            dma((8,)),
            dma((NY,)), dma((NY,)),
            dma((NX,)), dma((NX,)),
            dma((1,)), dma((1,)),
            dma((NR,)), dma((NR,)),
            dma((NC,)), dma((NC,)),
            dma((STEPS, 2, NSUB)), dma((STEPS, NSUB)), dma((STEPS, NSUB)),
        ],
        name="ladder_and_cycle",
        compiler_params=pltpu.CompilerParams(
            collective_id=0, has_side_effects=True, vmem_limit_bytes=60 << 20
        ),
    )(
        slab_amps, lad_pairs, cycle_dest.reshape(1, TILES), cycle_block, cycle_kblk,
        lad_ints, cycle_amps, cycle_ints,
    )


def solution(mesh):
    in_specs = (
        P("row", "col"),
        P(("row", "col"), None),
        P(("row", "col")),
        P(("row", "col"), None),
        P(("row", "col"), None),
        P(("row", "col")),
        P(("row", "col")),
        P("col", None),
    )
    out_specs = (P(None, ("row", "col")), P("row", "col"))
    return jax.shard_map(local, mesh=mesh, in_specs=in_specs, out_specs=out_specs, check_vma=False)
```

```python
import jax
import jax.numpy as jnp
from jax import lax
from jax.experimental import pallas as pl
from jax.experimental.pallas import tpu as pltpu
from jax.sharding import PartitionSpec as P

MESH = pl.DeviceIdType.MESH
F32 = jnp.float32
BF16 = jnp.bfloat16
I32 = jnp.int32

NR = 64
NC = 12
NY, NX = 8, 4
TILES = 64
ENTRIES = 384
Q_DEV = 24
MSG = 48
SUB = 64
NSUB = 4
STEPS = 6
JOIN = 4
LADDER_ORDER = (6, 5, 7, 4, 8, 3, 9, 2, 10, 1, 11)
LOW = 3
FIRST = 33
PLACED = 8


def dot(a, b):
    return jnp.dot(a, b, preferred_element_type=F32)


def iota(shape, dim):
    return lax.broadcasted_iota(I32, shape, dim)


def kernel(
    amps_hbm, pairs_hbm, dest_hbm, block_hbm, kblk_hbm, w_hbm, cyc_hbm, b_hbm,
    lad_out, cyc_out,
    amps_ref, pairs_ref, dest_ref, block_ref, kblk_ref,
    w_ref, cyc_ref, b_ref, stage, outgoing, arrived, gather, gstage, lad_lhs, placer, dense,
    lad_part, lad_low, lad_slots, cells, cyc_lhs, part, slot_up, slot_dn, low_out, low_in, turn, lines,
    local_sem, g1_send, g1_recv, g2_send, g2_recv, g3_send, g3_recv, a_send, a_recv, l_send, l_recv,
    r_send, r_recv_up, r_recv_dn,
):
    me = lax.axis_index("row")
    col = lax.axis_index("col")
    my_y = me // 8
    my_x = lax.rem(me // 2, 4)
    my_core = lax.rem(me, 2)

    barrier = pltpu.get_barrier_semaphore()

    def away(i):
        half = i // 2
        return 32 + half - 2 * half * lax.rem(i, 2)

    def greet_row(i, carry):
        pl.semaphore_signal(
            barrier, inc=1, device_id={"row": lax.rem(me + away(i), NR)}, device_id_type=MESH
        )
        return carry

    def greet_col(k, carry):
        pl.semaphore_signal(
            barrier, inc=1, device_id={"col": lax.rem(col + k, NC)}, device_id_type=MESH
        )
        return carry

    lax.fori_loop(1, NR, greet_row, 0)
    lax.fori_loop(1, NC, greet_col, 0)

    local = [
        pltpu.make_async_copy(cyc_hbm, cyc_ref, local_sem.at[0]),
        pltpu.make_async_copy(w_hbm, w_ref, local_sem.at[1]),
        pltpu.make_async_copy(b_hbm, b_ref, local_sem.at[2]),
        pltpu.make_async_copy(dest_hbm, dest_ref, local_sem.at[3]),
        pltpu.make_async_copy(block_hbm, block_ref, local_sem.at[4]),
        pltpu.make_async_copy(kblk_hbm, kblk_ref, local_sem.at[5]),
        pltpu.make_async_copy(amps_hbm, amps_ref, local_sem.at[6]),
        pltpu.make_async_copy(pairs_hbm, pairs_ref, local_sem.at[7]),
    ]
    for i in (3, 4, 5, 6, 0, 7, 1, 2):
        local[i].start()

    local[6].wait()
    for i in range(32):
        lines[i:i + 1, :] = amps_ref[:, i * 128:(i + 1) * 128].astype(F32)
    flipped = lines[...].T
    turn[:, 0:32] = flipped[0:64, :]
    turn[:, 32:64] = flipped[64:128, :]
    quarter = [[turn[pl.ds(2 * a1 + par, 16, stride=4), :] for a1 in (0, 1)] for par in (0, 1)]
    message = jnp.concatenate([jnp.concatenate(quarter[par], axis=1) for par in (0, 1)], axis=0)

    for i in (3, 4, 5):
        local[i].wait()
    dest_row = dest_ref[...]
    eye = iota((TILES, TILES), 0) == iota((TILES, TILES), 1)
    dest_col = jnp.sum(jnp.where(eye, dest_row, 0), axis=1, keepdims=True)
    same = dest_col == dest_row
    earlier_col = iota((TILES, TILES), 0) < iota((TILES, TILES), 1)
    earlier_row = iota((TILES, TILES), 1) < iota((TILES, TILES), 0)
    pos_row = jnp.sum(jnp.where(same & earlier_col, 1, 0), axis=0, keepdims=True)
    pos_col = jnp.sum(jnp.where(same & earlier_row, 1, 0), axis=1, keepdims=True)
    code_row = (block_ref[...] * 16 + kblk_ref[...]).reshape(1, TILES)
    code_col = jnp.sum(jnp.where(eye, code_row, 0), axis=1, keepdims=True)
    slot_row = dest_row * 2 + pos_row
    slot_col = dest_col * 2 + pos_col
    chosen = (iota((2 * NR, TILES), 0) == slot_row).astype(F32).astype(BF16)
    codes = jnp.sum(
        jnp.where(iota((TILES, 2 * NR), 1) == slot_col, code_col + 1, 0), axis=0, keepdims=True
    ) - 1
    gather[my_core, my_x, my_y, 0:32, :] = message.astype(BF16)
    gather[my_core, my_x, my_y, 32:48, :] = jnp.where(
        iota((16, 128), 0) == 0, codes, 0
    ).astype(F32).astype(BF16)

    local[0].wait()

    def stage_tiles(g, carry):
        picked = dot(chosen, cyc_ref[:, pl.ds(pl.multiple_of(g * 256, 256), 256)])
        stage[pl.ds(2 * g, 128, stride=32), :] = picked[:, 0:128]
        stage[pl.ds(2 * g + 1, 128, stride=32), :] = picked[:, 128:256]
        return carry

    lax.fori_loop(0, 16, stage_tiles, 0, unroll=4)

    def tile_fill(d, carry):
        outgoing[d] = stage[pl.ds(pl.multiple_of(d * 64, 64), 64), :].astype(BF16)
        return carry

    lax.fori_loop(0, NR, tile_fill, 0, unroll=4)
    arrived[me] = stage[pl.ds(pl.multiple_of(me * 64, 64), 64), :].astype(BF16)

    def tile_copy(d):
        return pltpu.make_async_remote_copy(
            outgoing.at[d], arrived.at[me], a_send.at[d], a_recv.at[me],
            device_id={"row": d}, device_id_type=MESH,
        )

    def tile_send(i, carry):
        tile_copy(lax.rem(me + away(i), NR)).start()
        return carry

    def first_copy(k, y):
        there = lax.rem(my_y + k, NY)
        ref = gather.at[my_core, my_x, y]
        return pltpu.make_async_remote_copy(
            ref, ref, g1_send.at[k], g1_recv.at[y],
            device_id={"row": there * 8 + my_x * 2 + my_core}, device_id_type=MESH,
        )

    def second_copy(k, x):
        there = lax.rem(my_x + k, NX)
        ref = gather.at[my_core, x]
        return pltpu.make_async_remote_copy(
            ref, ref, g2_send.at[k], g2_recv.at[x],
            device_id={"row": my_y * 8 + there * 2 + my_core}, device_id_type=MESH,
        )

    def third_copy(core):
        ref = gather.at[core]
        return pltpu.make_async_remote_copy(
            ref, ref, g3_send.at[0], g3_recv.at[0],
            device_id={"row": me + 1 - 2 * my_core}, device_id_type=MESH,
        )

    pl.semaphore_wait(barrier, NR - 1 + NC - 1)
    for k in (4, 3, 5, 2, 6, 1, 7):
        first_copy(k, my_y).start()
    lax.fori_loop(1, FIRST, tile_send, 0)

    local[7].wait()
    pairs = pairs_ref[...].reshape(1, ENTRIES)
    p_at = iota((64, ENTRIES), 0)
    p_code = (2 * lax.rem(p_at, 32) + p_at // 32) * Q_DEV

    def build(q, carry):
        placer[pl.ds(pl.multiple_of(q * 64, 64), 64), :] = (
            (p_code + q == pairs).astype(F32).astype(BF16)
        )
        return carry

    lax.fori_loop(0, Q_DEV, build, 0)
    local[1].wait()

    def place(g, carry):
        w_part = w_ref[:, pl.ds(pl.multiple_of(g * 256, 256), 256)]
        for quarter_at in range(4):
            placed = dot(placer[quarter_at * 384:(quarter_at + 1) * 384, :], w_part).astype(BF16)
            for j in range(6):
                q = quarter_at * 6 + j
                for i in (0, 1):
                    dense[
                        q // 2, pl.ds(pl.multiple_of((2 * g + i) * 64, 64), 64),
                        (q % 2) * 128:(q % 2 + 1) * 128,
                    ] = placed[j * 64:(j + 1) * 64, i * 128:(i + 1) * 128]
        return carry

    lax.fori_loop(0, PLACED, place, 0, unroll=2)

    for k in range(1, NY):
        first_copy(k, lax.rem(my_y + k, NY)).wait_recv()
    for k in (2, 1, 3):
        second_copy(k, my_x).start()
    lax.fori_loop(FIRST, NR, tile_send, 0)
    lax.fori_loop(PLACED, 16, place, 0, unroll=2)
    for k in range(1, NX):
        second_copy(k, lax.rem(my_x + k, NX)).wait_recv()
    third_copy(my_core).start()
    third_copy(1 - my_core).wait_recv()

    def widen(i, carry):
        core, x, y = i // 32, lax.rem(i // 8, NX), lax.rem(i, NY)
        row = y * 8 + x * 2 + core
        gstage[pl.ds(pl.multiple_of(row * MSG, MSG), MSG), :] = gather[core, x, y].astype(F32)
        return carry

    lax.fori_loop(0, NR, widen, 0, unroll=4)
    for par in (0, 1):
        for b in range(16):
            lad_lhs[par * 64:(par + 1) * 64, b * 128:(b + 1) * 128] = (
                gstage[pl.ds(par * 16 + b, NR, stride=MSG), :].astype(BF16)
            )

    low = iota((64, 128), 1) < 64

    def lad_copy(k):
        c = lax.rem(col + k, NC)
        return pltpu.make_async_remote_copy(
            lad_low.at[c], lad_slots.at[k], l_send.at[k], l_recv.at[k],
            device_id={"col": c}, device_id_type=MESH,
        )

    def ladder(k):
        c = lax.rem(col + k, NC)
        acc = dot(lad_lhs[...], dense[c])
        first = acc[0:64, 0:128] + pltpu.roll(acc[64:128, 0:128], 64, 1)
        second = pltpu.roll(acc[0:64, 128:256], 64, 1) + acc[64:128, 128:256]
        total = jnp.where(low, first, second)
        if k == 0:
            lad_part[...] = total
        else:
            lad_low[c] = total.astype(BF16)

    def ladder_send(k):
        ladder(k)
        lad_copy(k).start()

    for k in LADDER_ORDER:
        ladder_send(k)
    ladder(0)

    all_codes = gstage[pl.ds(32, NR, stride=MSG), :]
    mine = []
    for j in (0, 1):
        here = jnp.where(iota((NR, 128), 1) == 2 * me + j, all_codes, 0.0)
        mine.append(jnp.sum(here, axis=1, keepdims=True))
    slot_codes = jnp.concatenate(mine, axis=0)
    put = (slot_codes == iota((2 * NR, 128), 1).astype(F32)).astype(F32).T[0:64, :].astype(BF16)

    def tile_wait(i, carry):
        k = away(i)
        s = lax.rem(me + NR - k, NR)
        pltpu.make_async_remote_copy(
            outgoing.at[s], arrived.at[s], a_send.at[s], a_recv.at[s],
            device_id={"row": lax.rem(me + k, NR)}, device_id_type=MESH,
        ).wait_recv()
        stage[pl.ds(pl.multiple_of(s * 64, 64), 64), :] = arrived[s].astype(F32)
        return carry

    stage[pl.ds(pl.multiple_of(me * 64, 64), 64), :] = arrived[me].astype(F32)
    lax.fori_loop(1, NR, tile_wait, 0)

    def cell(g, carry):
        wide = []
        for i in (0, 1):
            a = 2 * g + i
            wide.append(jnp.concatenate(
                [stage[pl.ds(a + 32 * j, NR, stride=64), :] for j in (0, 1)], axis=0
            ).astype(BF16))
        summed = dot(put, jnp.concatenate(wide, axis=1))
        cells[pl.ds(2 * g, 64, stride=32), :] = summed[:, 0:128]
        cells[pl.ds(2 * g + 1, 64, stride=32), :] = summed[:, 128:256]
        return carry

    lax.fori_loop(0, 16, cell, 0, unroll=8)

    low32 = iota((32, 128), 1) < 64

    def pair(i, carry):
        m, nn = i // 8, lax.rem(i, 8)
        at = pl.multiple_of((m * 16 + 2 * nn) * 32, 32)
        even = cells[pl.ds(at, 32), :]
        odd = cells[pl.ds(pl.multiple_of(at + 32, 32), 32), :]
        lanes = pl.ds(pl.multiple_of(nn * 128, 128), 128)
        cyc_lhs[pl.ds(pl.multiple_of(m * 32, 32), 32), lanes] = jnp.where(
            low32, even, pltpu.roll(odd, 64, 1)
        ).astype(BF16)
        cyc_lhs[pl.ds(pl.multiple_of(128 + m * 32, 32), 32), lanes] = jnp.where(
            low32, pltpu.roll(even, 64, 1), odd
        ).astype(BF16)
        return carry

    lax.fori_loop(0, 32, pair, 0, unroll=8)
    local[2].wait()

    def product(c):
        lanes = pl.ds(pl.multiple_of(c * 128, 128), 128)
        made = dot(cyc_lhs[...], b_ref[:, lanes])
        for u in range(NSUB):
            part[c, u] = made[u * SUB:(u + 1) * SUB, :]

    arms = ((slot_up, r_recv_up), (slot_dn, r_recv_dn))

    def target(t, arm):
        return lax.rem(col + (STEPS - t if arm == 0 else NC - STEPS + t), NC)

    def pieces(t, arm):
        if t:
            return range(NSUB)
        return (0, 1) if arm == 0 else (2, 3)

    def ring_copy(t, arm, u):
        hop = max(STEPS - t - JOIN, 1)
        device = lax.rem(col + (hop if arm == 0 else NC - hop), NC)
        slots, recv = arms[arm]
        if t < LOW:
            source, landing = low_out.at[t, arm, u], low_in.at[t, arm, u]
        else:
            source, landing = part.at[target(t, arm), u], slots.at[t - LOW, u]
        return pltpu.make_async_remote_copy(
            source, landing, r_send.at[t, arm, u], recv.at[t, u],
            device_id={"col": device}, device_id_type=MESH,
        )

    def ring_send(t, arm, u):
        if t < LOW:
            low_out[t, arm, u] = part[target(t, arm), u].astype(BF16)
        ring_copy(t, arm, u).start()

    def landed(t, arm, u):
        ring_copy(t, arm, u).wait_recv()
        return low_in[t, arm, u].astype(F32) if t < LOW else arms[arm][0][t - LOW, u]

    product(target(0, 0))
    for arm in (0, 1):
        for u in pieces(0, arm):
            ring_send(0, arm, u)
    for t in range(1, STEPS):
        for arm in (0, 1):
            product(target(t, arm))
        for i in range(NSUB):
            for arm in (0, 1):
                u = i if arm == 0 else (i + 2) % 4
                c = target(t, arm)
                came = range(t) if t == STEPS - JOIN else (t - 1,) if t > STEPS - JOIN else ()
                for past in came:
                    if u in pieces(past, arm):
                        part[c, u] = part[c, u] + landed(past, arm, u)
                ring_send(t, arm, u)
    product(col)

    def lad_wait(k, carry):
        lad_copy(k).wait_recv()
        return carry

    lax.fori_loop(1, NC, lad_wait, 0)
    total = lad_part[...]
    for k in range(1, NC):
        total = total + lad_slots[k].astype(F32)
    lad_out[...] = total

    for u in range(NSUB):
        par, half = u // 2, u % 2
        cyc_out[pl.ds(par + half * 128, SUB, stride=2), :] = (
            part[col, u] + landed(STEPS - 1, 0, u) + landed(STEPS - 1, 1, u)
        )

    def tile_sent(k, carry):
        tile_copy(lax.rem(me + k, NR)).wait_send()
        return carry

    def lad_sent(k, carry):
        lad_copy(k).wait_send()
        return carry

    for k in range(1, NY):
        first_copy(k, my_y).wait_send()
    for k in range(1, NX):
        second_copy(k, my_x).wait_send()
    third_copy(my_core).wait_send()
    lax.fori_loop(1, NR, tile_sent, 0)
    lax.fori_loop(1, NC, lad_sent, 0)
    for t in range(STEPS):
        for arm in (0, 1):
            for u in pieces(t, arm):
                ring_copy(t, arm, u).wait_send()


def local(
    slab_amps, lad_ints, lad_pairs, cycle_amps, cycle_dest, cycle_block, cycle_kblk, cycle_ints
):
    vmem = pl.BlockSpec(memory_space=pltpu.VMEM)
    hbm = pl.BlockSpec(memory_space=pl.ANY)
    dma = pltpu.SemaphoreType.DMA
    return pl.pallas_call(
        kernel,
        out_shape=(
            jax.ShapeDtypeStruct((64, 128), F32),
            jax.ShapeDtypeStruct((256, 128), F32),
        ),
        in_specs=[hbm] * 8,
        out_specs=(vmem, vmem),
        scratch_shapes=[
            pltpu.VMEM((1, 4096), BF16),
            pltpu.VMEM((ENTRIES,), I32),
            pltpu.VMEM((1, TILES), I32),
            pltpu.VMEM((TILES,), I32),
            pltpu.VMEM((TILES,), I32),
            pltpu.VMEM((ENTRIES, 4096), BF16),
            pltpu.VMEM((TILES, 4096), BF16),
            pltpu.VMEM((1024, 1536), BF16),
            pltpu.VMEM((4096, 128), F32),
            pltpu.VMEM((NR, 64, 128), BF16),
            pltpu.VMEM((NR, 64, 128), BF16),
            pltpu.VMEM((2, NX, NY, MSG, 128), BF16),
            pltpu.VMEM((NR * MSG, 128), F32),
            pltpu.VMEM((128, 2048), BF16),
            pltpu.VMEM((Q_DEV * 64, ENTRIES), BF16),
            pltpu.VMEM((NC, 2048, 256), BF16),
            pltpu.VMEM((64, 128), F32),
            pltpu.VMEM((NC, 64, 128), BF16),
            pltpu.VMEM((NC, 64, 128), BF16),
            pltpu.VMEM((2048, 128), F32),
            pltpu.VMEM((256, 1024), BF16),
            pltpu.VMEM((NC, NSUB, SUB, 128), F32),
            pltpu.VMEM((STEPS - LOW, NSUB, SUB, 128), F32),
            pltpu.VMEM((STEPS - LOW, NSUB, SUB, 128), F32),
            pltpu.VMEM((max(LOW, 1), 2, NSUB, SUB, 128), BF16),
            pltpu.VMEM((max(LOW, 1), 2, NSUB, SUB, 128), BF16),
            pltpu.VMEM((64, 64), F32),
            pltpu.VMEM((32, 128), F32),
            dma((8,)),
            dma((NY,)), dma((NY,)),
            dma((NX,)), dma((NX,)),
            dma((1,)), dma((1,)),
            dma((NR,)), dma((NR,)),
            dma((NC,)), dma((NC,)),
            dma((STEPS, 2, NSUB)), dma((STEPS, NSUB)), dma((STEPS, NSUB)),
        ],
        name="ladder_and_cycle",
        compiler_params=pltpu.CompilerParams(
            collective_id=0, has_side_effects=True, vmem_limit_bytes=60 << 20
        ),
    )(
        slab_amps, lad_pairs, cycle_dest.reshape(1, TILES), cycle_block, cycle_kblk,
        lad_ints, cycle_amps, cycle_ints,
    )


def solution(mesh):
    in_specs = (
        P("row", "col"),
        P(("row", "col"), None),
        P(("row", "col")),
        P(("row", "col"), None),
        P(("row", "col"), None),
        P(("row", "col")),
        P(("row", "col")),
        P("col", None),
    )
    out_specs = (P(None, ("row", "col")), P("row", "col"))
    return jax.shard_map(local, mesh=mesh, in_specs=in_specs, out_specs=out_specs, check_vma=False)
```

```python
import jax
import jax.numpy as jnp
from jax import lax
from jax.experimental import pallas as pl
from jax.experimental.pallas import tpu as pltpu
from jax.sharding import PartitionSpec as P

MESH = pl.DeviceIdType.MESH
F32 = jnp.float32
BF16 = jnp.bfloat16
I32 = jnp.int32

NR = 64
NC = 12
NY, NX = 8, 4
TILES = 64
ENTRIES = 384
Q_DEV = 24
MSG = 48
SUB = 64
NSUB = 4
STEPS = 6
JOIN = 4
LADDER_ORDER = (6, 5, 7, 4, 8, 3, 9, 2, 10, 1, 11)
LOW = 3
FIRST = 33
PLACED = 8


def dot(a, b):
    return jnp.dot(a, b, preferred_element_type=F32)


def iota(shape, dim):
    return lax.broadcasted_iota(I32, shape, dim)


def kernel(
    amps_hbm, pairs_hbm, dest_hbm, block_hbm, kblk_hbm, w_hbm, cyc_hbm, b_hbm,
    lad_out, cyc_out,
    amps_ref, pairs_ref, dest_ref, block_ref, kblk_ref,
    w_ref, cyc_ref, b_ref, stage, outgoing, arrived, gather, gstage, lad_lhs, placer, dense,
    lad_part, lad_low, lad_slots, cells, cyc_lhs, part, slot_up, slot_dn, low_out, low_in, turn, lines,
    local_sem, g1_send, g1_recv, g2_send, g2_recv, g3_send, g3_recv, a_send, a_recv, l_send, l_recv,
    r_send, r_recv_up, r_recv_dn,
):
    me = lax.axis_index("row")
    col = lax.axis_index("col")
    my_y = me // 8
    my_x = lax.rem(me // 2, 4)
    my_core = lax.rem(me, 2)

    barrier = pltpu.get_barrier_semaphore()

    def away(i):
        half = i // 2
        return 32 + half - 2 * half * lax.rem(i, 2)

    def greet_row(i, carry):
        pl.semaphore_signal(
            barrier, inc=1, device_id={"row": lax.rem(me + away(i), NR)}, device_id_type=MESH
        )
        return carry

    def greet_col(k, carry):
        pl.semaphore_signal(
            barrier, inc=1, device_id={"col": lax.rem(col + k, NC)}, device_id_type=MESH
        )
        return carry

    lax.fori_loop(1, NR, greet_row, 0, unroll=7)
    lax.fori_loop(1, NC, greet_col, 0)

    local = [
        pltpu.make_async_copy(cyc_hbm, cyc_ref, local_sem.at[0]),
        pltpu.make_async_copy(w_hbm, w_ref, local_sem.at[1]),
        pltpu.make_async_copy(b_hbm, b_ref, local_sem.at[2]),
        pltpu.make_async_copy(dest_hbm, dest_ref, local_sem.at[3]),
        pltpu.make_async_copy(block_hbm, block_ref, local_sem.at[4]),
        pltpu.make_async_copy(kblk_hbm, kblk_ref, local_sem.at[5]),
        pltpu.make_async_copy(amps_hbm, amps_ref, local_sem.at[6]),
        pltpu.make_async_copy(pairs_hbm, pairs_ref, local_sem.at[7]),
    ]
    for i in (3, 4, 5, 6, 0, 7, 1, 2):
        local[i].start()

    local[6].wait()
    for i in range(32):
        lines[i:i + 1, :] = amps_ref[:, i * 128:(i + 1) * 128].astype(F32)
    flipped = lines[...].T
    turn[:, 0:32] = flipped[0:64, :]
    turn[:, 32:64] = flipped[64:128, :]
    quarter = [[turn[pl.ds(2 * a1 + par, 16, stride=4), :] for a1 in (0, 1)] for par in (0, 1)]
    message = jnp.concatenate([jnp.concatenate(quarter[par], axis=1) for par in (0, 1)], axis=0)

    for i in (3, 4, 5):
        local[i].wait()
    dest_row = dest_ref[...]
    eye = iota((TILES, TILES), 0) == iota((TILES, TILES), 1)
    dest_col = jnp.sum(jnp.where(eye, dest_row, 0), axis=1, keepdims=True)
    same = dest_col == dest_row
    earlier_col = iota((TILES, TILES), 0) < iota((TILES, TILES), 1)
    earlier_row = iota((TILES, TILES), 1) < iota((TILES, TILES), 0)
    pos_row = jnp.sum(jnp.where(same & earlier_col, 1, 0), axis=0, keepdims=True)
    pos_col = jnp.sum(jnp.where(same & earlier_row, 1, 0), axis=1, keepdims=True)
    code_row = (block_ref[...] * 16 + kblk_ref[...]).reshape(1, TILES)
    code_col = jnp.sum(jnp.where(eye, code_row, 0), axis=1, keepdims=True)
    slot_row = dest_row * 2 + pos_row
    slot_col = dest_col * 2 + pos_col
    chosen = (iota((2 * NR, TILES), 0) == slot_row).astype(F32).astype(BF16)
    codes = jnp.sum(
        jnp.where(iota((TILES, 2 * NR), 1) == slot_col, code_col + 1, 0), axis=0, keepdims=True
    ) - 1
    gather[my_core, my_x, my_y, 0:32, :] = message.astype(BF16)
    gather[my_core, my_x, my_y, 32:48, :] = jnp.where(
        iota((16, 128), 0) == 0, codes, 0
    ).astype(F32).astype(BF16)

    local[0].wait()

    def stage_tiles(g, carry):
        picked = dot(chosen, cyc_ref[:, pl.ds(pl.multiple_of(g * 256, 256), 256)])
        stage[pl.ds(2 * g, 128, stride=32), :] = picked[:, 0:128]
        stage[pl.ds(2 * g + 1, 128, stride=32), :] = picked[:, 128:256]
        return carry

    lax.fori_loop(0, 16, stage_tiles, 0, unroll=4)

    def tile_fill(d, carry):
        outgoing[d] = stage[pl.ds(pl.multiple_of(d * 64, 64), 64), :].astype(BF16)
        return carry

    lax.fori_loop(0, NR, tile_fill, 0, unroll=4)
    arrived[me] = stage[pl.ds(pl.multiple_of(me * 64, 64), 64), :].astype(BF16)

    def tile_copy(d):
        return pltpu.make_async_remote_copy(
            outgoing.at[d], arrived.at[me], a_send.at[d], a_recv.at[me],
            device_id={"row": d}, device_id_type=MESH,
        )

    def tile_send(i, carry):
        tile_copy(lax.rem(me + away(i), NR)).start()
        return carry

    def first_copy(k, y):
        there = lax.rem(my_y + k, NY)
        ref = gather.at[my_core, my_x, y]
        return pltpu.make_async_remote_copy(
            ref, ref, g1_send.at[k], g1_recv.at[y],
            device_id={"row": there * 8 + my_x * 2 + my_core}, device_id_type=MESH,
        )

    def second_copy(k, x):
        there = lax.rem(my_x + k, NX)
        ref = gather.at[my_core, x]
        return pltpu.make_async_remote_copy(
            ref, ref, g2_send.at[k], g2_recv.at[x],
            device_id={"row": my_y * 8 + there * 2 + my_core}, device_id_type=MESH,
        )

    def third_copy(core):
        ref = gather.at[core]
        return pltpu.make_async_remote_copy(
            ref, ref, g3_send.at[0], g3_recv.at[0],
            device_id={"row": me + 1 - 2 * my_core}, device_id_type=MESH,
        )

    pl.semaphore_wait(barrier, NR - 1 + NC - 1)
    for k in (4, 3, 5, 2, 6, 1, 7):
        first_copy(k, my_y).start()
    lax.fori_loop(1, FIRST, tile_send, 0)

    local[7].wait()
    pairs = pairs_ref[...].reshape(1, ENTRIES)
    p_at = iota((64, ENTRIES), 0)
    p_code = (2 * lax.rem(p_at, 32) + p_at // 32) * Q_DEV

    def build(q, carry):
        placer[pl.ds(pl.multiple_of(q * 64, 64), 64), :] = (
            (p_code + q == pairs).astype(F32).astype(BF16)
        )
        return carry

    lax.fori_loop(0, Q_DEV, build, 0, unroll=4)
    local[1].wait()

    def place(g, carry):
        w_part = w_ref[:, pl.ds(pl.multiple_of(g * 256, 256), 256)]
        for quarter_at in range(4):
            placed = dot(placer[quarter_at * 384:(quarter_at + 1) * 384, :], w_part).astype(BF16)
            for j in range(6):
                q = quarter_at * 6 + j
                for i in (0, 1):
                    dense[
                        q // 2, pl.ds(pl.multiple_of((2 * g + i) * 64, 64), 64),
                        (q % 2) * 128:(q % 2 + 1) * 128,
                    ] = placed[j * 64:(j + 1) * 64, i * 128:(i + 1) * 128]
        return carry

    lax.fori_loop(0, PLACED, place, 0, unroll=2)

    for k in range(1, NY):
        first_copy(k, lax.rem(my_y + k, NY)).wait_recv()
    for k in (2, 1, 3):
        second_copy(k, my_x).start()
    lax.fori_loop(FIRST, NR, tile_send, 0)
    lax.fori_loop(PLACED, 16, place, 0, unroll=2)
    for k in range(1, NX):
        second_copy(k, lax.rem(my_x + k, NX)).wait_recv()
    third_copy(my_core).start()
    third_copy(1 - my_core).wait_recv()

    def widen(i, carry):
        core, x, y = i // 32, lax.rem(i // 8, NX), lax.rem(i, NY)
        row = y * 8 + x * 2 + core
        gstage[pl.ds(pl.multiple_of(row * MSG, MSG), MSG), :] = gather[core, x, y].astype(F32)
        return carry

    lax.fori_loop(0, NR, widen, 0, unroll=4)
    for par in (0, 1):
        for b in range(16):
            lad_lhs[par * 64:(par + 1) * 64, b * 128:(b + 1) * 128] = (
                gstage[pl.ds(par * 16 + b, NR, stride=MSG), :].astype(BF16)
            )

    low = iota((64, 128), 1) < 64

    def lad_copy(k):
        c = lax.rem(col + k, NC)
        return pltpu.make_async_remote_copy(
            lad_low.at[c], lad_slots.at[k], l_send.at[k], l_recv.at[k],
            device_id={"col": c}, device_id_type=MESH,
        )

    def ladder(k):
        c = lax.rem(col + k, NC)
        acc = dot(lad_lhs[...], dense[c])
        first = acc[0:64, 0:128] + pltpu.roll(acc[64:128, 0:128], 64, 1)
        second = pltpu.roll(acc[0:64, 128:256], 64, 1) + acc[64:128, 128:256]
        total = jnp.where(low, first, second)
        if k == 0:
            lad_part[...] = total
        else:
            lad_low[c] = total.astype(BF16)

    def ladder_send(k):
        ladder(k)
        lad_copy(k).start()

    for k in LADDER_ORDER:
        ladder_send(k)
    ladder(0)

    all_codes = gstage[pl.ds(32, NR, stride=MSG), :]
    mine = []
    for j in (0, 1):
        here = jnp.where(iota((NR, 128), 1) == 2 * me + j, all_codes, 0.0)
        mine.append(jnp.sum(here, axis=1, keepdims=True))
    slot_codes = jnp.concatenate(mine, axis=0)
    put = (slot_codes == iota((2 * NR, 128), 1).astype(F32)).astype(F32).T[0:64, :].astype(BF16)

    def tile_wait(i, carry):
        k = away(i)
        s = lax.rem(me + NR - k, NR)
        pltpu.make_async_remote_copy(
            outgoing.at[s], arrived.at[s], a_send.at[s], a_recv.at[s],
            device_id={"row": lax.rem(me + k, NR)}, device_id_type=MESH,
        ).wait_recv()
        stage[pl.ds(pl.multiple_of(s * 64, 64), 64), :] = arrived[s].astype(F32)
        return carry

    stage[pl.ds(pl.multiple_of(me * 64, 64), 64), :] = arrived[me].astype(F32)
    lax.fori_loop(1, NR, tile_wait, 0, unroll=3)

    def cell(g, carry):
        wide = []
        for i in (0, 1):
            a = 2 * g + i
            wide.append(jnp.concatenate(
                [stage[pl.ds(a + 32 * j, NR, stride=64), :] for j in (0, 1)], axis=0
            ).astype(BF16))
        summed = dot(put, jnp.concatenate(wide, axis=1))
        cells[pl.ds(2 * g, 64, stride=32), :] = summed[:, 0:128]
        cells[pl.ds(2 * g + 1, 64, stride=32), :] = summed[:, 128:256]
        return carry

    lax.fori_loop(0, 16, cell, 0, unroll=8)

    low32 = iota((32, 128), 1) < 64

    def pair(i, carry):
        m, nn = i // 8, lax.rem(i, 8)
        at = pl.multiple_of((m * 16 + 2 * nn) * 32, 32)
        even = cells[pl.ds(at, 32), :]
        odd = cells[pl.ds(pl.multiple_of(at + 32, 32), 32), :]
        lanes = pl.ds(pl.multiple_of(nn * 128, 128), 128)
        cyc_lhs[pl.ds(pl.multiple_of(m * 32, 32), 32), lanes] = jnp.where(
            low32, even, pltpu.roll(odd, 64, 1)
        ).astype(BF16)
        cyc_lhs[pl.ds(pl.multiple_of(128 + m * 32, 32), 32), lanes] = jnp.where(
            low32, pltpu.roll(even, 64, 1), odd
        ).astype(BF16)
        return carry

    lax.fori_loop(0, 32, pair, 0, unroll=8)
    local[2].wait()

    def product(c):
        lanes = pl.ds(pl.multiple_of(c * 128, 128), 128)
        made = dot(cyc_lhs[...], b_ref[:, lanes])
        for u in range(NSUB):
            part[c, u] = made[u * SUB:(u + 1) * SUB, :]

    arms = ((slot_up, r_recv_up), (slot_dn, r_recv_dn))

    def target(t, arm):
        return lax.rem(col + (STEPS - t if arm == 0 else NC - STEPS + t), NC)

    def pieces(t, arm):
        if t:
            return range(NSUB)
        return (0, 1) if arm == 0 else (2, 3)

    def ring_copy(t, arm, u):
        hop = max(STEPS - t - JOIN, 1)
        device = lax.rem(col + (hop if arm == 0 else NC - hop), NC)
        slots, recv = arms[arm]
        if t < LOW:
            source, landing = low_out.at[t, arm, u], low_in.at[t, arm, u]
        else:
            source, landing = part.at[target(t, arm), u], slots.at[t - LOW, u]
        return pltpu.make_async_remote_copy(
            source, landing, r_send.at[t, arm, u], recv.at[t, u],
            device_id={"col": device}, device_id_type=MESH,
        )

    def ring_send(t, arm, u):
        if t < LOW:
            low_out[t, arm, u] = part[target(t, arm), u].astype(BF16)
        ring_copy(t, arm, u).start()

    def landed(t, arm, u):
        ring_copy(t, arm, u).wait_recv()
        return low_in[t, arm, u].astype(F32) if t < LOW else arms[arm][0][t - LOW, u]

    product(target(0, 0))
    for arm in (0, 1):
        for u in pieces(0, arm):
            ring_send(0, arm, u)
    for t in range(1, STEPS):
        for arm in (0, 1):
            product(target(t, arm))
        for i in range(NSUB):
            for arm in (0, 1):
                u = i if arm == 0 else (i + 2) % 4
                c = target(t, arm)
                came = range(t) if t == STEPS - JOIN else (t - 1,) if t > STEPS - JOIN else ()
                for past in came:
                    if u in pieces(past, arm):
                        part[c, u] = part[c, u] + landed(past, arm, u)
                ring_send(t, arm, u)
    product(col)

    def lad_wait(k, carry):
        lad_copy(k).wait_recv()
        return carry

    lax.fori_loop(1, NC, lad_wait, 0)
    total = lad_part[...]
    for k in range(1, NC):
        total = total + lad_slots[k].astype(F32)
    lad_out[...] = total

    def tile_sent(k, carry):
        tile_copy(lax.rem(me + k, NR)).wait_send()
        return carry

    def lad_sent(k, carry):
        lad_copy(k).wait_send()
        return carry

    for k in range(1, NY):
        first_copy(k, my_y).wait_send()
    for k in range(1, NX):
        second_copy(k, my_x).wait_send()
    third_copy(my_core).wait_send()
    lax.fori_loop(1, NR, tile_sent, 0)
    lax.fori_loop(1, NC, lad_sent, 0)
    for u in range(NSUB):
        par, half = u // 2, u % 2
        cyc_out[pl.ds(par + half * 128, SUB, stride=2), :] = (
            part[col, u] + landed(STEPS - 1, 0, u) + landed(STEPS - 1, 1, u)
        )

    for t in range(STEPS):
        for arm in (0, 1):
            for u in pieces(t, arm):
                ring_copy(t, arm, u).wait_send()


def local(
    slab_amps, lad_ints, lad_pairs, cycle_amps, cycle_dest, cycle_block, cycle_kblk, cycle_ints
):
    vmem = pl.BlockSpec(memory_space=pltpu.VMEM)
    hbm = pl.BlockSpec(memory_space=pl.ANY)
    dma = pltpu.SemaphoreType.DMA
    return pl.pallas_call(
        kernel,
        out_shape=(
            jax.ShapeDtypeStruct((64, 128), F32),
            jax.ShapeDtypeStruct((256, 128), F32),
        ),
        in_specs=[hbm] * 8,
        out_specs=(vmem, vmem),
        scratch_shapes=[
            pltpu.VMEM((1, 4096), BF16),
            pltpu.VMEM((ENTRIES,), I32),
            pltpu.VMEM((1, TILES), I32),
            pltpu.VMEM((TILES,), I32),
            pltpu.VMEM((TILES,), I32),
            pltpu.VMEM((ENTRIES, 4096), BF16),
            pltpu.VMEM((TILES, 4096), BF16),
            pltpu.VMEM((1024, 1536), BF16),
            pltpu.VMEM((4096, 128), F32),
            pltpu.VMEM((NR, 64, 128), BF16),
            pltpu.VMEM((NR, 64, 128), BF16),
            pltpu.VMEM((2, NX, NY, MSG, 128), BF16),
            pltpu.VMEM((NR * MSG, 128), F32),
            pltpu.VMEM((128, 2048), BF16),
            pltpu.VMEM((Q_DEV * 64, ENTRIES), BF16),
            pltpu.VMEM((NC, 2048, 256), BF16),
            pltpu.VMEM((64, 128), F32),
            pltpu.VMEM((NC, 64, 128), BF16),
            pltpu.VMEM((NC, 64, 128), BF16),
            pltpu.VMEM((2048, 128), F32),
            pltpu.VMEM((256, 1024), BF16),
            pltpu.VMEM((NC, NSUB, SUB, 128), F32),
            pltpu.VMEM((STEPS - LOW, NSUB, SUB, 128), F32),
            pltpu.VMEM((STEPS - LOW, NSUB, SUB, 128), F32),
            pltpu.VMEM((max(LOW, 1), 2, NSUB, SUB, 128), BF16),
            pltpu.VMEM((max(LOW, 1), 2, NSUB, SUB, 128), BF16),
            pltpu.VMEM((64, 64), F32),
            pltpu.VMEM((32, 128), F32),
            dma((8,)),
            dma((NY,)), dma((NY,)),
            dma((NX,)), dma((NX,)),
            dma((1,)), dma((1,)),
            dma((NR,)), dma((NR,)),
            dma((NC,)), dma((NC,)),
            dma((STEPS, 2, NSUB)), dma((STEPS, NSUB)), dma((STEPS, NSUB)),
        ],
        name="ladder_and_cycle",
        compiler_params=pltpu.CompilerParams(
            collective_id=0, has_side_effects=True, vmem_limit_bytes=60 << 20
        ),
    )(
        slab_amps, lad_pairs, cycle_dest.reshape(1, TILES), cycle_block, cycle_kblk,
        lad_ints, cycle_amps, cycle_ints,
    )


def solution(mesh):
    in_specs = (
        P("row", "col"),
        P(("row", "col"), None),
        P(("row", "col")),
        P(("row", "col"), None),
        P(("row", "col"), None),
        P(("row", "col")),
        P(("row", "col")),
        P("col", None),
    )
    out_specs = (P(None, ("row", "col")), P("row", "col"))
    return jax.shard_map(local, mesh=mesh, in_specs=in_specs, out_specs=out_specs, check_vma=False)
```

```python
import jax
import jax.numpy as jnp
from jax import lax
from jax.experimental import pallas as pl
from jax.experimental.pallas import tpu as pltpu
from jax.sharding import PartitionSpec as P

MESH = pl.DeviceIdType.MESH
F32 = jnp.float32
BF16 = jnp.bfloat16
I32 = jnp.int32

NR = 64
NC = 12
NY, NX = 8, 4
TILES = 64
ENTRIES = 384
Q_DEV = 24
MSG = 48
SUB = 64
NSUB = 4
STEPS = 6
JOIN = 4
LADDER_ORDER = (6, 5, 7, 4, 8, 3, 9, 2, 10, 1, 11)
LOW = 3
FIRST = 33
PLACED = 8


def dot(a, b):
    return jnp.dot(a, b, preferred_element_type=F32)


def iota(shape, dim):
    return lax.broadcasted_iota(I32, shape, dim)


def kernel(
    amps_hbm, pairs_hbm, dest_hbm, block_hbm, kblk_hbm, w_hbm, cyc_hbm, b_hbm,
    lad_out, cyc_out,
    amps_ref, pairs_ref, dest_ref, block_ref, kblk_ref,
    w_ref, cyc_ref, b_ref, stage, outgoing, arrived, gather, gstage, lad_lhs, placer, dense,
    lad_part, lad_low, lad_slots, cells, cyc_lhs, part, slot_up, slot_dn, low_out, low_in, turn, lines,
    local_sem, g1_send, g1_recv, g2_send, g2_recv, g3_send, g3_recv, a_send, a_recv, l_send, l_recv,
    r_send, r_recv_up, r_recv_dn,
):
    me = lax.axis_index("row")
    col = lax.axis_index("col")
    my_y = me // 8
    my_x = lax.rem(me // 2, 4)
    my_core = lax.rem(me, 2)

    barrier = pltpu.get_barrier_semaphore()

    def away(i):
        half = i // 2
        return 32 + half - 2 * half * lax.rem(i, 2)

    def greet_row(i, carry):
        pl.semaphore_signal(
            barrier, inc=1, device_id={"row": lax.rem(me + away(i), NR)}, device_id_type=MESH
        )
        return carry

    def greet_col(k, carry):
        pl.semaphore_signal(
            barrier, inc=1, device_id={"col": lax.rem(col + k, NC)}, device_id_type=MESH
        )
        return carry

    lax.fori_loop(1, NR, greet_row, 0, unroll=7)
    lax.fori_loop(1, NC, greet_col, 0)

    local = [
        pltpu.make_async_copy(cyc_hbm, cyc_ref, local_sem.at[0]),
        pltpu.make_async_copy(w_hbm, w_ref, local_sem.at[1]),
        pltpu.make_async_copy(b_hbm, b_ref, local_sem.at[2]),
        pltpu.make_async_copy(dest_hbm, dest_ref, local_sem.at[3]),
        pltpu.make_async_copy(block_hbm, block_ref, local_sem.at[4]),
        pltpu.make_async_copy(kblk_hbm, kblk_ref, local_sem.at[5]),
        pltpu.make_async_copy(amps_hbm, amps_ref, local_sem.at[6]),
        pltpu.make_async_copy(pairs_hbm, pairs_ref, local_sem.at[7]),
    ]
    for i in (3, 4, 5, 6, 0, 7, 1, 2):
        local[i].start()

    local[6].wait()
    for i in range(32):
        lines[i:i + 1, :] = amps_ref[:, i * 128:(i + 1) * 128].astype(F32)
    flipped = lines[...].T
    turn[:, 0:32] = flipped[0:64, :]
    turn[:, 32:64] = flipped[64:128, :]
    quarter = [[turn[pl.ds(2 * a1 + par, 16, stride=4), :] for a1 in (0, 1)] for par in (0, 1)]
    message = jnp.concatenate([jnp.concatenate(quarter[par], axis=1) for par in (0, 1)], axis=0)

    for i in (3, 4, 5):
        local[i].wait()
    dest_row = dest_ref[...]
    eye = iota((TILES, TILES), 0) == iota((TILES, TILES), 1)
    dest_col = jnp.sum(jnp.where(eye, dest_row, 0), axis=1, keepdims=True)
    same = dest_col == dest_row
    earlier_col = iota((TILES, TILES), 0) < iota((TILES, TILES), 1)
    earlier_row = iota((TILES, TILES), 1) < iota((TILES, TILES), 0)
    pos_row = jnp.sum(jnp.where(same & earlier_col, 1, 0), axis=0, keepdims=True)
    pos_col = jnp.sum(jnp.where(same & earlier_row, 1, 0), axis=1, keepdims=True)
    code_row = (block_ref[...] * 16 + kblk_ref[...]).reshape(1, TILES)
    code_col = jnp.sum(jnp.where(eye, code_row, 0), axis=1, keepdims=True)
    slot_row = dest_row * 2 + pos_row
    slot_col = dest_col * 2 + pos_col
    chosen = (iota((2 * NR, TILES), 0) == slot_row).astype(F32).astype(BF16)
    codes = jnp.sum(
        jnp.where(iota((TILES, 2 * NR), 1) == slot_col, code_col + 1, 0), axis=0, keepdims=True
    ) - 1
    gather[my_core, my_x, my_y, 0:32, :] = message.astype(BF16)
    gather[my_core, my_x, my_y, 32:48, :] = jnp.where(
        iota((16, 128), 0) == 0, codes, 0
    ).astype(F32).astype(BF16)

    local[0].wait()

    def stage_tiles(g, carry):
        picked = dot(chosen, cyc_ref[:, pl.ds(pl.multiple_of(g * 256, 256), 256)])
        stage[pl.ds(2 * g, 128, stride=32), :] = picked[:, 0:128]
        stage[pl.ds(2 * g + 1, 128, stride=32), :] = picked[:, 128:256]
        return carry

    lax.fori_loop(0, 16, stage_tiles, 0, unroll=4)

    def tile_fill(d, carry):
        outgoing[d] = stage[pl.ds(pl.multiple_of(d * 64, 64), 64), :].astype(BF16)
        return carry

    lax.fori_loop(0, NR, tile_fill, 0, unroll=4)
    arrived[me] = stage[pl.ds(pl.multiple_of(me * 64, 64), 64), :].astype(BF16)

    def tile_copy(d):
        return pltpu.make_async_remote_copy(
            outgoing.at[d], arrived.at[me], a_send.at[d], a_recv.at[me],
            device_id={"row": d}, device_id_type=MESH,
        )

    def tile_send(i, carry):
        tile_copy(lax.rem(me + away(i), NR)).start()
        return carry

    def first_copy(k, y):
        there = lax.rem(my_y + k, NY)
        ref = gather.at[my_core, my_x, y]
        return pltpu.make_async_remote_copy(
            ref, ref, g1_send.at[k], g1_recv.at[y],
            device_id={"row": there * 8 + my_x * 2 + my_core}, device_id_type=MESH,
        )

    def second_copy(k, x):
        there = lax.rem(my_x + k, NX)
        ref = gather.at[my_core, x]
        return pltpu.make_async_remote_copy(
            ref, ref, g2_send.at[k], g2_recv.at[x],
            device_id={"row": my_y * 8 + there * 2 + my_core}, device_id_type=MESH,
        )

    def third_copy(core):
        ref = gather.at[core]
        return pltpu.make_async_remote_copy(
            ref, ref, g3_send.at[0], g3_recv.at[0],
            device_id={"row": me + 1 - 2 * my_core}, device_id_type=MESH,
        )

    pl.semaphore_wait(barrier, NR - 1 + NC - 1)
    for k in (4, 3, 5, 2, 6, 1, 7):
        first_copy(k, my_y).start()
    lax.fori_loop(1, FIRST, tile_send, 0)

    local[7].wait()
    pairs = pairs_ref[...].reshape(1, ENTRIES)
    p_at = iota((64, ENTRIES), 0)
    p_code = (2 * lax.rem(p_at, 32) + p_at // 32) * Q_DEV

    def build(q, carry):
        placer[pl.ds(pl.multiple_of(q * 64, 64), 64), :] = (
            (p_code + q == pairs).astype(F32).astype(BF16)
        )
        return carry

    lax.fori_loop(0, Q_DEV, build, 0, unroll=4)
    local[1].wait()

    def place(g, carry):
        w_part = w_ref[:, pl.ds(pl.multiple_of(g * 256, 256), 256)]
        for quarter_at in range(4):
            placed = dot(placer[quarter_at * 384:(quarter_at + 1) * 384, :], w_part).astype(BF16)
            for j in range(6):
                q = quarter_at * 6 + j
                for i in (0, 1):
                    dense[
                        q // 2, pl.ds(pl.multiple_of((2 * g + i) * 64, 64), 64),
                        (q % 2) * 128:(q % 2 + 1) * 128,
                    ] = placed[j * 64:(j + 1) * 64, i * 128:(i + 1) * 128]
        return carry

    lax.fori_loop(0, PLACED, place, 0, unroll=2)

    for k in range(1, NY):
        first_copy(k, lax.rem(my_y + k, NY)).wait_recv()
    for k in (2, 1, 3):
        second_copy(k, my_x).start()
    lax.fori_loop(FIRST, NR, tile_send, 0)
    lax.fori_loop(PLACED, 16, place, 0, unroll=2)
    for k in range(1, NX):
        second_copy(k, lax.rem(my_x + k, NX)).wait_recv()
    third_copy(my_core).start()
    third_copy(1 - my_core).wait_recv()

    def widen(i, carry):
        core, x, y = i // 32, lax.rem(i // 8, NX), lax.rem(i, NY)
        row = y * 8 + x * 2 + core
        gstage[pl.ds(pl.multiple_of(row * MSG, MSG), MSG), :] = gather[core, x, y].astype(F32)
        return carry

    lax.fori_loop(0, NR, widen, 0, unroll=4)
    for par in (0, 1):
        for b in range(16):
            lad_lhs[par * 64:(par + 1) * 64, b * 128:(b + 1) * 128] = (
                gstage[pl.ds(par * 16 + b, NR, stride=MSG), :].astype(BF16)
            )

    low = iota((64, 128), 1) < 64

    def lad_copy(k):
        c = lax.rem(col + k, NC)
        return pltpu.make_async_remote_copy(
            lad_low.at[c], lad_slots.at[k], l_send.at[k], l_recv.at[k],
            device_id={"col": c}, device_id_type=MESH,
        )

    def ladder(k):
        c = lax.rem(col + k, NC)
        acc = dot(lad_lhs[...], dense[c])
        first = acc[0:64, 0:128] + pltpu.roll(acc[64:128, 0:128], 64, 1)
        second = pltpu.roll(acc[0:64, 128:256], 64, 1) + acc[64:128, 128:256]
        total = jnp.where(low, first, second)
        if k == 0:
            lad_part[...] = total
        else:
            lad_low[c] = total.astype(BF16)

    def ladder_send(k):
        ladder(k)
        lad_copy(k).start()

    for k in LADDER_ORDER:
        ladder_send(k)

    all_codes = gstage[pl.ds(32, NR, stride=MSG), :]
    mine = []
    for j in (0, 1):
        here = jnp.where(iota((NR, 128), 1) == 2 * me + j, all_codes, 0.0)
        mine.append(jnp.sum(here, axis=1, keepdims=True))
    slot_codes = jnp.concatenate(mine, axis=0)
    put = (slot_codes == iota((2 * NR, 128), 1).astype(F32)).astype(F32).T[0:64, :].astype(BF16)

    def tile_wait(i, carry):
        k = away(i)
        s = lax.rem(me + NR - k, NR)
        pltpu.make_async_remote_copy(
            outgoing.at[s], arrived.at[s], a_send.at[s], a_recv.at[s],
            device_id={"row": lax.rem(me + k, NR)}, device_id_type=MESH,
        ).wait_recv()
        stage[pl.ds(pl.multiple_of(s * 64, 64), 64), :] = arrived[s].astype(F32)
        return carry

    stage[pl.ds(pl.multiple_of(me * 64, 64), 64), :] = arrived[me].astype(F32)
    lax.fori_loop(1, NR, tile_wait, 0, unroll=3)

    def cell(g, carry):
        wide = []
        for i in (0, 1):
            a = 2 * g + i
            wide.append(jnp.concatenate(
                [stage[pl.ds(a + 32 * j, NR, stride=64), :] for j in (0, 1)], axis=0
            ).astype(BF16))
        summed = dot(put, jnp.concatenate(wide, axis=1))
        cells[pl.ds(2 * g, 64, stride=32), :] = summed[:, 0:128]
        cells[pl.ds(2 * g + 1, 64, stride=32), :] = summed[:, 128:256]
        return carry

    lax.fori_loop(0, 16, cell, 0, unroll=16)

    low32 = iota((32, 128), 1) < 64

    def pair(i, carry):
        m, nn = i // 8, lax.rem(i, 8)
        at = pl.multiple_of((m * 16 + 2 * nn) * 32, 32)
        even = cells[pl.ds(at, 32), :]
        odd = cells[pl.ds(pl.multiple_of(at + 32, 32), 32), :]
        lanes = pl.ds(pl.multiple_of(nn * 128, 128), 128)
        cyc_lhs[pl.ds(pl.multiple_of(m * 32, 32), 32), lanes] = jnp.where(
            low32, even, pltpu.roll(odd, 64, 1)
        ).astype(BF16)
        cyc_lhs[pl.ds(pl.multiple_of(128 + m * 32, 32), 32), lanes] = jnp.where(
            low32, pltpu.roll(even, 64, 1), odd
        ).astype(BF16)
        return carry

    lax.fori_loop(0, 32, pair, 0, unroll=8)
    local[2].wait()

    def product(c):
        lanes = pl.ds(pl.multiple_of(c * 128, 128), 128)
        made = dot(cyc_lhs[...], b_ref[:, lanes])
        for u in range(NSUB):
            part[c, u] = made[u * SUB:(u + 1) * SUB, :]

    arms = ((slot_up, r_recv_up), (slot_dn, r_recv_dn))

    def target(t, arm):
        return lax.rem(col + (STEPS - t if arm == 0 else NC - STEPS + t), NC)

    def pieces(t, arm):
        if t:
            return range(NSUB)
        return (0, 1) if arm == 0 else (2, 3)

    def ring_copy(t, arm, u):
        hop = max(STEPS - t - JOIN, 1)
        device = lax.rem(col + (hop if arm == 0 else NC - hop), NC)
        slots, recv = arms[arm]
        if t < LOW:
            source, landing = low_out.at[t, arm, u], low_in.at[t, arm, u]
        else:
            source, landing = part.at[target(t, arm), u], slots.at[t - LOW, u]
        return pltpu.make_async_remote_copy(
            source, landing, r_send.at[t, arm, u], recv.at[t, u],
            device_id={"col": device}, device_id_type=MESH,
        )

    def ring_send(t, arm, u):
        if t < LOW:
            low_out[t, arm, u] = part[target(t, arm), u].astype(BF16)
        ring_copy(t, arm, u).start()

    def landed(t, arm, u):
        ring_copy(t, arm, u).wait_recv()
        return low_in[t, arm, u].astype(F32) if t < LOW else arms[arm][0][t - LOW, u]

    product(target(0, 0))
    for arm in (0, 1):
        for u in pieces(0, arm):
            ring_send(0, arm, u)
    for t in range(1, STEPS):
        for arm in (0, 1):
            product(target(t, arm))
        for i in range(NSUB):
            for arm in (0, 1):
                u = i if arm == 0 else (i + 2) % 4
                c = target(t, arm)
                came = range(t) if t == STEPS - JOIN else (t - 1,) if t > STEPS - JOIN else ()
                for past in came:
                    if u in pieces(past, arm):
                        part[c, u] = part[c, u] + landed(past, arm, u)
                ring_send(t, arm, u)
    product(col)

    def lad_wait(k, carry):
        lad_copy(k).wait_recv()
        return carry

    lax.fori_loop(1, NC, lad_wait, 0)
    ladder(0)
    total = lad_part[...]
    for k in range(1, NC):
        total = total + lad_slots[k].astype(F32)
    lad_out[...] = total

    def tile_sent(k, carry):
        tile_copy(lax.rem(me + k, NR)).wait_send()
        return carry

    def lad_sent(k, carry):
        lad_copy(k).wait_send()
        return carry

    for k in range(1, NY):
        first_copy(k, my_y).wait_send()
    for k in range(1, NX):
        second_copy(k, my_x).wait_send()
    third_copy(my_core).wait_send()
    lax.fori_loop(1, NR, tile_sent, 0)
    lax.fori_loop(1, NC, lad_sent, 0)
    for u in range(NSUB):
        par, half = u // 2, u % 2
        cyc_out[pl.ds(par + half * 128, SUB, stride=2), :] = (
            part[col, u] + landed(STEPS - 1, 0, u) + landed(STEPS - 1, 1, u)
        )

    for t in range(STEPS):
        for arm in (0, 1):
            for u in pieces(t, arm):
                ring_copy(t, arm, u).wait_send()


def local(
    slab_amps, lad_ints, lad_pairs, cycle_amps, cycle_dest, cycle_block, cycle_kblk, cycle_ints
):
    vmem = pl.BlockSpec(memory_space=pltpu.VMEM)
    hbm = pl.BlockSpec(memory_space=pl.ANY)
    dma = pltpu.SemaphoreType.DMA
    return pl.pallas_call(
        kernel,
        out_shape=(
            jax.ShapeDtypeStruct((64, 128), F32),
            jax.ShapeDtypeStruct((256, 128), F32),
        ),
        in_specs=[hbm] * 8,
        out_specs=(vmem, vmem),
        scratch_shapes=[
            pltpu.VMEM((1, 4096), BF16),
            pltpu.VMEM((ENTRIES,), I32),
            pltpu.VMEM((1, TILES), I32),
            pltpu.VMEM((TILES,), I32),
            pltpu.VMEM((TILES,), I32),
            pltpu.VMEM((ENTRIES, 4096), BF16),
            pltpu.VMEM((TILES, 4096), BF16),
            pltpu.VMEM((1024, 1536), BF16),
            pltpu.VMEM((4096, 128), F32),
            pltpu.VMEM((NR, 64, 128), BF16),
            pltpu.VMEM((NR, 64, 128), BF16),
            pltpu.VMEM((2, NX, NY, MSG, 128), BF16),
            pltpu.VMEM((NR * MSG, 128), F32),
            pltpu.VMEM((128, 2048), BF16),
            pltpu.VMEM((Q_DEV * 64, ENTRIES), BF16),
            pltpu.VMEM((NC, 2048, 256), BF16),
            pltpu.VMEM((64, 128), F32),
            pltpu.VMEM((NC, 64, 128), BF16),
            pltpu.VMEM((NC, 64, 128), BF16),
            pltpu.VMEM((2048, 128), F32),
            pltpu.VMEM((256, 1024), BF16),
            pltpu.VMEM((NC, NSUB, SUB, 128), F32),
            pltpu.VMEM((STEPS - LOW, NSUB, SUB, 128), F32),
            pltpu.VMEM((STEPS - LOW, NSUB, SUB, 128), F32),
            pltpu.VMEM((max(LOW, 1), 2, NSUB, SUB, 128), BF16),
            pltpu.VMEM((max(LOW, 1), 2, NSUB, SUB, 128), BF16),
            pltpu.VMEM((64, 64), F32),
            pltpu.VMEM((32, 128), F32),
            dma((8,)),
            dma((NY,)), dma((NY,)),
            dma((NX,)), dma((NX,)),
            dma((1,)), dma((1,)),
            dma((NR,)), dma((NR,)),
            dma((NC,)), dma((NC,)),
            dma((STEPS, 2, NSUB)), dma((STEPS, NSUB)), dma((STEPS, NSUB)),
        ],
        name="ladder_and_cycle",
        compiler_params=pltpu.CompilerParams(
            collective_id=0, has_side_effects=True, vmem_limit_bytes=60 << 20
        ),
    )(
        slab_amps, lad_pairs, cycle_dest.reshape(1, TILES), cycle_block, cycle_kblk,
        lad_ints, cycle_amps, cycle_ints,
    )


def solution(mesh):
    in_specs = (
        P("row", "col"),
        P(("row", "col"), None),
        P(("row", "col")),
        P(("row", "col"), None),
        P(("row", "col"), None),
        P(("row", "col")),
        P(("row", "col")),
        P("col", None),
    )
    out_specs = (P(None, ("row", "col")), P("row", "col"))
    return jax.shard_map(local, mesh=mesh, in_specs=in_specs, out_specs=out_specs, check_vma=False)
```
